512 devices in a mesh: brick: 64 (over z, x), chan: 8 (over y, core).
Axes of the slice: x: 4, y: 4, z: 16, core: 2. Of those that a mesh axis runs over, the one named last changes fastest.
Arguments:
- features: bfloat16 [512, 96, 512], P(('brick', 'chan')), may hold values from -6 to 6
- occupancy: int32 [512, 512], P(('brick', 'chan')), may hold values from 0 to 1
- neighbors: int32 [512, 27], P(('brick', 'chan')), may hold values from -1 to 511, as said below
- weight: bfloat16 [27, 96, 96], replicated, may hold values from -0.125 to 0.125
- grad_output: bfloat16 [512, 96, 512], P(('brick', 'chan')), may hold values from -6 to 6
Outputs:
- output: bfloat16 [512, 96, 512], P(('brick', 'chan'))
- grad_features: bfloat16 [512, 96, 512], P(('brick', 'chan'))
- grad_weight: float32 [27, 96, 96], replicated
The draws below stay inside these ranges and needn't reach their ends.
Inputs may be any that keep to these rules, and one draw needn't show every extreme that they name: `neighbors`: column 13 holds the brick's own index. Every other entry is -1 or a brick held by the same device or the one just below or above it along brick+chan (1 bricks a device, in order).
All inputs are finite; a program needn't handle non-finite values.
Results may differ from the reference program's by a relative error of at most 0.0055.
Values may be sent and summed in bfloat16 or wider, within the bound.
No kernel may reach another device: no remote copies, remote signals or barrier semaphores. Data moves between devices by JAX's collectives and lax.ppermute only.
A program may use at most 64 MiB of HBM per device.

```python
import jax
import jax.numpy as jnp
from jax import lax

C = 96
B_DEV = 1
NB = 512


def draw_occupancy(key, part):
    key = jax.random.fold_in(key, 11)
    first_key, second_key = jax.random.split(key)
    levels = jax.random.randint(first_key, (NB, 1), 1, 10)
    rolled = jax.random.randint(second_key, (NB, 512), 0, 10)
    return (rolled < levels).astype(jnp.int32)


def draw_neighbors(key, part):
    key = jax.random.fold_in(key, 23)
    subkeys = jax.random.split(key, 3)
    devices = NB // B_DEV
    owner_dev = (jnp.arange(NB) // B_DEV)[:, None]
    stride_dev = jax.random.randint(subkeys[0], (NB, 27), -1, 2)
    target = jnp.clip(owner_dev + stride_dev, 0, devices - 1)
    chosen = jax.random.randint(subkeys[1], (NB, 27), 0, B_DEV)
    present = jax.random.randint(subkeys[2], (NB, 27), 0, 4) < 3
    result = jnp.where(present, target * B_DEV + chosen, -1)
    result = result.at[:, 13].set(jnp.arange(NB))
    return result.astype(jnp.int32)


def steps_of(stream_key, dims, pieces, smallest, largest):
    factor_of, own = 1.0, jax.random.fold_in(stream_key, 6)
    for axis_at, parts in pieces:
        draws = jnp.exp(jax.random.uniform(jax.random.fold_in(own, axis_at), (parts,), jnp.float32, smallest / len(pieces), largest / len(pieces)))
        factor_of = factor_of * jnp.repeat(draws, dims[axis_at] // parts).reshape([-1 if axis == axis_at else 1 for axis in range(len(dims))])
    return factor_of


def gaussian(rng, dims, width, reach, cuts=(), kind=jnp.bfloat16):
    level = steps_of(rng, dims, cuts, -0.22, 0.18) if cuts else 1.0
    values = jax.random.normal(rng, dims, jnp.float32) * width * level
    return jnp.minimum(jnp.maximum(values, -reach), reach).astype(kind)


def setup_inputs(seed: int = 0) -> dict:
    streams_of = jax.random.split(jax.random.key(seed), 6)
    return {
        "features": gaussian(streams_of[0], (NB, C, 512), 1.0, 6.0, ((0, 512),)),
        "occupancy": draw_occupancy(jax.random.fold_in(streams_of[5], 71), 0),
        "neighbors": draw_neighbors(jax.random.fold_in(streams_of[5], 71), 0),
        "weight": gaussian(streams_of[3], (27, C, C), (27 * C) ** -0.5, 0.125),
        "grad_output": gaussian(streams_of[4], (NB, C, 512), 1.0, 6.0, ((0, 512),)),
    }


OFFSETS = [(dx, dy, dz) for dx in (-1, 0, 1) for dy in (-1, 0, 1) for dz in (-1, 0, 1)]


def region(stride):
    if stride < 0:
        return slice(7, 8), slice(0, 1)
    if stride > 0:
        return slice(0, 1), slice(9, 10)
    return slice(0, 8), slice(1, 9)


def assemble(source, lookup):
    number = lookup.shape[0]
    depth = source.shape[1]
    cubes = source.reshape(source.shape[0], depth, 8, 8, 8)
    padded = jnp.zeros((number, depth, 10, 10, 10), source.dtype)
    for offset_id, shift in enumerate(OFFSETS):
        src_x, dst_x = region(shift[0])
        src_y, dst_y = region(shift[1])
        src_z, dst_z = region(shift[2])
        slab = cubes[:, :, src_x, src_y, src_z]
        picked = jnp.take(slab, lookup[:, offset_id], axis=0)
        padded = padded.at[:, :, dst_x, dst_y, dst_z].set(picked)
    return padded


def disperse(grads, lookup, total):
    depth = grads.shape[1]
    buffer = jnp.zeros((total + 1, depth, 8, 8, 8), jnp.float32)
    for offset_id, shift in enumerate(OFFSETS):
        src_x, dst_x = region(shift[0])
        src_y, dst_y = region(shift[1])
        src_z, dst_z = region(shift[2])
        buffer = buffer.at[lookup[:, offset_id], :, src_x, src_y, src_z].add(grads[:, :, dst_x, dst_y, dst_z])
    return buffer[:total]


def reference(features, occupancy, neighbors, weight, grad_output):
    total = features.shape[0]
    depth = features.shape[1]
    occ_float = occupancy.reshape(total, 1, 512).astype(jnp.float32)
    masked = features * occupancy.reshape(total, 1, 512).astype(jnp.bfloat16)
    source = jnp.concatenate([masked, jnp.zeros((1, depth, 512), jnp.bfloat16)], axis=0)
    lookup = jnp.where(neighbors >= 0, neighbors, total).astype(jnp.int32)
    padded = assemble(source, lookup).astype(jnp.float32)
    kernel = weight.astype(jnp.float32)
    cotangent = (grad_output * occupancy.reshape(total, 1, 512).astype(jnp.bfloat16)).astype(jnp.float32)
    summed = jnp.zeros((total, depth, 512), jnp.float32)
    grad_padded = jnp.zeros((total, depth, 10, 10, 10), jnp.float32)
    tap_grads = []
    for tap, shift in enumerate(OFFSETS):
        low_x, low_y, low_z = shift[0] + 1, shift[1] + 1, shift[2] + 1
        window = padded[:, :, low_x:low_x + 8, low_y:low_y + 8, low_z:low_z + 8].reshape(total, depth, 512)
        summed = summed + jnp.einsum("co,bcv->bov", kernel[tap], window, precision=lax.Precision.HIGHEST)
        back = jnp.einsum("co,bov->bcv", kernel[tap], cotangent, precision=lax.Precision.HIGHEST)
        grad_padded = grad_padded.at[:, :, low_x:low_x + 8, low_y:low_y + 8, low_z:low_z + 8].add(back.reshape(total, depth, 8, 8, 8))
        tap_grads.append(jnp.einsum("bcv,bov->co", window, cotangent, precision=lax.Precision.HIGHEST))
    output = (summed * occ_float).astype(jnp.bfloat16)
    grad_source = disperse(grad_padded, lookup, total).reshape(total, depth, 512)
    grad_features = (grad_source * occ_float).astype(jnp.bfloat16)
    grad_weight = jnp.stack(tap_grads, axis=0)
    return output, grad_features, grad_weight
```

```python
import jax
import jax.numpy as jnp
from jax import lax
from jax.experimental import pallas as pl
from jax.experimental.pallas import tpu as pltpu
from jax.sharding import PartitionSpec as P

AXES = ("brick", "chan")
SIGNS = (-1, 0, 1)
VOXELS, LANES, CODES = 512, 128, 32
VMEM = pl.BlockSpec(memory_space=pltpu.VMEM)
SMEM = pl.BlockSpec(memory_space=pltpu.SMEM)
LIMIT = 32 * 1024 * 1024


def voxel_rows(block, occupied):
    masked = block.astype(jnp.float32) * occupied
    spare = jnp.zeros((LANES - masked.shape[0], masked.shape[1]), jnp.float32)
    return jnp.concatenate([masked, spare], axis=0).T


def pack_kernel(neighbors, occupancy, features, grad_output, cotangent, masked):
    occupied = occupancy[...].astype(jnp.float32)
    cotangent[:VOXELS, :] = voxel_rows(grad_output[0], occupied).astype(jnp.bfloat16)
    masked[...] = voxel_rows(features[0], occupied).astype(jnp.bfloat16)
    own = neighbors[0, 13]
    row = lax.broadcasted_iota(jnp.int32, (CODES, LANES), 0)
    codes = jnp.full((CODES, LANES), 2, jnp.int32)
    for offset in range(27):
        brick = neighbors[0, offset]
        codes = jnp.where(row == offset, jnp.where(brick < 0, 2, brick - own), codes)
    cotangent[VOXELS:, :] = codes.astype(jnp.float32).astype(jnp.bfloat16)


def faces(sign):
    if sign < 0:
        return slice(7, 8), slice(0, 1)
    if sign > 0:
        return slice(0, 1), slice(9, 10)
    return slice(0, 8), slice(1, 9)


def offset_id(x, y, z):
    return 9 * (x + 1) + 3 * (y + 1) + (z + 1)


def build_windows(bricks, own, weigh, columns, windows):
    for x in SIGNS:
        from_x, to_x = faces(x)
        for y in SIGNS:
            from_y, to_y = faces(y)
            parts = [brick[from_x, from_y] for brick in bricks]
            shape = parts[0].shape

            def side(z):
                return sum(part * scale for part, scale in zip(parts, weigh(x, y, z)))

            middle = parts[own] if x == 0 and y == 0 else side(0)
            middle = middle.reshape(-1, 8, LANES)
            below = side(-1).reshape(-1, 8, LANES)
            above = side(1).reshape(-1, 8, LANES)
            row = lax.broadcasted_iota(jnp.int32, middle.shape, 1)
            columns[0, to_x, to_y] = pltpu.roll(jnp.where(row == 7, below, middle), 1, 1).reshape(shape)
            columns[1, to_x, to_y] = middle.reshape(shape)
            columns[2, to_x, to_y] = pltpu.roll(jnp.where(row == 0, above, middle), 7, 1).reshape(shape)
    for dy in range(3):
        for dz in range(3):
            tap = 3 * dy + dz
            for px in range(10):
                windows[px, :, tap * LANES:(tap + 1) * LANES] = (
                    columns[dz, px, dy:dy + 8].reshape(64, LANES).astype(jnp.bfloat16)
                )


def rows_of(ref):
    return ref[:VOXELS, :].astype(jnp.float32).reshape(8, 8, 8, LANES)


def returned_scales(own, before, after):
    tables = [ref[VOXELS:, :].astype(jnp.float32) for ref in (before, own, after)]

    def weigh(x, y, z):
        at = offset_id(-x, -y, -z)
        return [
            jnp.where(table[at:at + 1] == code, 1.0, 0.0)
            for table, code in zip(tables, (1.0, 0.0, -1.0))
        ]

    return weigh


def read_scales(own):
    table = own[VOXELS:, :].astype(jnp.float32)

    def weigh(x, y, z):
        at = offset_id(x, y, z)
        return [jnp.where(table[at:at + 1] == code, 1.0, 0.0) for code in (-1.0, 0.0, 1.0)]

    return weigh


def span(windows, dx):
    return windows[dx:dx + 8].reshape(VOXELS, 9 * LANES)


def weight_grad_kernel(features, occupancy, own, before, after, grad, columns, windows):
    depth = features.shape[1]
    bricks = [rows_of(ref) for ref in (before, own, after)]
    build_windows(bricks, 1, returned_scales(own, before, after), columns, windows)
    masked = (features[0].astype(jnp.float32) * occupancy[...].astype(jnp.float32)).astype(jnp.bfloat16)
    for dx in range(3):
        product = jnp.dot(masked, span(windows, dx), preferred_element_type=jnp.float32)
        for tap in range(9):
            grad[26 - (9 * dx + tap)] = product[:, tap * LANES:tap * LANES + depth].astype(grad.dtype)


def outputs_kernel(
    occupancy, weight, own, before, after, masked, masked_before, masked_after,
    output, grad_features, columns, windows, taps,
):
    depth = weight.shape[1]
    occupied = occupancy[...].astype(jnp.float32)
    taps[...] = jnp.zeros_like(taps)
    for tap in range(27):
        taps[tap, :depth, :depth] = weight[tap]

    def finish(rows):
        return (rows.T[:depth] * occupied).astype(jnp.bfloat16)

    bricks = [rows_of(ref) for ref in (masked_before, masked, masked_after)]
    build_windows(bricks, 1, read_scales(own), columns, windows)
    total = jnp.zeros((VOXELS, LANES), jnp.float32)
    for dx in range(3):
        kernel = taps[9 * dx:9 * dx + 9].reshape(9 * LANES, LANES)
        total = total + jnp.dot(span(windows, dx), kernel, preferred_element_type=jnp.float32)
    output[0] = finish(total)

    bricks = [rows_of(ref) for ref in (before, own, after)]
    build_windows(bricks, 1, returned_scales(own, before, after), columns, windows)
    total = jnp.zeros((VOXELS, LANES), jnp.float32)
    for dx in range(3):
        for tap in range(9):
            total = total + lax.dot_general(
                windows[dx:dx + 8, :, tap * LANES:(tap + 1) * LANES].reshape(VOXELS, LANES),
                taps[26 - (9 * dx + tap)],
                (((1,), (1,)), ((), ())),
                preferred_element_type=jnp.float32,
            )
    grad_features[0] = finish(total)


WINDOW_SCRATCH = [
    pltpu.VMEM((3, 10, 10, 8, LANES), jnp.float32),
    pltpu.VMEM((10, 64, 9 * LANES), jnp.bfloat16),
]


def both_ways(block):
    count = lax.axis_size("brick") * lax.axis_size("chan")
    before = lax.ppermute(block, AXES, [(i, i + 1) for i in range(count - 1)])
    after = lax.ppermute(block, AXES, [(i + 1, i) for i in range(count - 1)])
    return before, after


def total_over_devices(grad):
    return lax.psum(grad, AXES)


def shards(features, occupancy, neighbors, weight, grad_output):
    depth = features.shape[1]
    cotangent, masked = pl.pallas_call(
        pack_kernel,
        out_shape=[
            jax.ShapeDtypeStruct((VOXELS + CODES, LANES), jnp.bfloat16),
            jax.ShapeDtypeStruct((VOXELS, LANES), jnp.bfloat16),
        ],
        in_specs=[SMEM, VMEM, VMEM, VMEM],
        out_specs=[VMEM, VMEM],
        name="pack",
    )(neighbors, occupancy, features, grad_output)
    before, after = both_ways(cotangent)
    masked_before, masked_after = both_ways(masked)
    grad = pl.pallas_call(
        weight_grad_kernel,
        out_shape=jax.ShapeDtypeStruct((27, depth, depth), jnp.float32),
        in_specs=[VMEM] * 5,
        out_specs=VMEM,
        scratch_shapes=WINDOW_SCRATCH,
        compiler_params=pltpu.CompilerParams(vmem_limit_bytes=LIMIT),
        cost_estimate=pl.CostEstimate(flops=27 * 2 * 128 * 128 * 512, bytes_accessed=2 * 1024 * 1024, transcendentals=0),
        name="weight_grad",
    )(features, occupancy, cotangent, before, after)
    grad_weight = total_over_devices(grad)
    output, grad_features = pl.pallas_call(
        outputs_kernel,
        out_shape=[jax.ShapeDtypeStruct(features.shape, jnp.bfloat16)] * 2,
        in_specs=[VMEM] * 8,
        out_specs=[VMEM, VMEM],
        scratch_shapes=WINDOW_SCRATCH + [pltpu.VMEM((27, LANES, LANES), jnp.bfloat16)],
        compiler_params=pltpu.CompilerParams(vmem_limit_bytes=LIMIT),
        cost_estimate=pl.CostEstimate(flops=54 * 2 * 128 * 128 * 512, bytes_accessed=2 * 1024 * 1024, transcendentals=0),
        name="outputs",
    )(occupancy, weight, cotangent, before, after, masked, masked_before, masked_after)
    return output, grad_features, grad_weight


def solution(mesh):
    split = P(AXES, None, None)
    flat = P(AXES, None)
    return jax.shard_map(
        shards,
        mesh=mesh,
        in_specs=(split, flat, flat, P(), split),
        out_specs=(split, split, P()),
        check_vma=False,
    )
```

```python
import jax
import jax.numpy as jnp
from jax import lax
from jax.experimental import pallas as pl
from jax.experimental.pallas import tpu as pltpu
from jax.sharding import PartitionSpec as P

AXES = ("brick", "chan")
SIGNS = (-1, 0, 1)
VOXELS, LANES, CODES = 512, 128, 32
ROWS = 2048
NEAR, FAR = 64, 8
VMEM = pl.BlockSpec(memory_space=pltpu.VMEM)
SMEM = pl.BlockSpec(memory_space=pltpu.SMEM)
LIMIT = 32 * 1024 * 1024


def voxel_rows(block, occupied):
    masked = block.astype(jnp.float32) * occupied
    spare = jnp.zeros((LANES - masked.shape[0], masked.shape[1]), jnp.float32)
    return jnp.concatenate([masked, spare], axis=0).T


def pack_kernel(neighbors, occupancy, features, grad_output, packed):
    occupied = occupancy[...].astype(jnp.float32)
    packed[:VOXELS, :] = voxel_rows(grad_output[0], occupied).astype(jnp.bfloat16)
    packed[VOXELS:2 * VOXELS, :] = voxel_rows(features[0], occupied).astype(jnp.bfloat16)
    own = neighbors[0, 13]
    row = lax.broadcasted_iota(jnp.int32, (CODES, LANES), 0)
    codes = jnp.full((CODES, LANES), 2, jnp.int32)
    for offset in range(27):
        brick = neighbors[0, offset]
        codes = jnp.where(row == offset, jnp.where(brick < 0, 2, brick - own), codes)
    packed[2 * VOXELS:, :] = codes.astype(jnp.float32).astype(jnp.bfloat16)


def faces(sign):
    if sign < 0:
        return slice(7, 8), slice(0, 1)
    if sign > 0:
        return slice(0, 1), slice(9, 10)
    return slice(0, 8), slice(1, 9)


def offset_id(x, y, z):
    return 9 * (x + 1) + 3 * (y + 1) + (z + 1)


def build_windows(bricks, own, weigh, columns, windows):
    for x in SIGNS:
        from_x, to_x = faces(x)
        for y in SIGNS:
            from_y, to_y = faces(y)
            parts = [brick[from_x, from_y] for brick in bricks]
            shape = parts[0].shape

            def side(z):
                return sum(part * scale for part, scale in zip(parts, weigh(x, y, z)))

            middle = parts[own] if x == 0 and y == 0 else side(0)
            middle = middle.reshape(-1, 8, LANES)
            below = side(-1).reshape(-1, 8, LANES)
            above = side(1).reshape(-1, 8, LANES)
            row = lax.broadcasted_iota(jnp.int32, middle.shape, 1)
            columns[0, to_x, to_y] = pltpu.roll(jnp.where(row == 7, below, middle), 1, 1).reshape(shape)
            columns[1, to_x, to_y] = middle.reshape(shape)
            columns[2, to_x, to_y] = pltpu.roll(jnp.where(row == 0, above, middle), 7, 1).reshape(shape)
    for dy in range(3):
        for dz in range(3):
            tap = 3 * dy + dz
            for px in range(10):
                windows[px, :, tap * LANES:(tap + 1) * LANES] = (
                    columns[dz, px, dy:dy + 8].reshape(64, LANES).astype(jnp.bfloat16)
                )


def cotangent_of(ref):
    return ref[:VOXELS, :].astype(jnp.float32).reshape(8, 8, 8, LANES)


def masked_of(ref):
    return ref[VOXELS:2 * VOXELS, :].astype(jnp.float32).reshape(8, 8, 8, LANES)


def codes_of(ref):
    return ref[2 * VOXELS:, :].astype(jnp.float32)


def returned_scales(own, before, after):
    tables = [codes_of(ref) for ref in (before, own, after)]

    def weigh(x, y, z):
        at = offset_id(-x, -y, -z)
        return [
            jnp.where(table[at:at + 1] == code, 1.0, 0.0)
            for table, code in zip(tables, (1.0, 0.0, -1.0))
        ]

    return weigh


def read_scales(own):
    table = codes_of(own)

    def weigh(x, y, z):
        at = offset_id(x, y, z)
        return [jnp.where(table[at:at + 1] == code, 1.0, 0.0) for code in (-1.0, 0.0, 1.0)]

    return weigh


def span(windows, dx):
    return windows[dx:dx + 8].reshape(VOXELS, 9 * LANES)


def dense_rows(block):
    lane = lax.broadcasted_iota(jnp.int32, (72, LANES), 1)
    tail = jnp.concatenate([pltpu.roll(block[72:], 96 - 32 * third, 1) for third in range(3)], axis=0)
    return jnp.where(lane < 96, block[:72], tail)


def square_rows(dense):
    lane = lax.broadcasted_iota(jnp.int32, (24, LANES), 1)
    thirds = [pltpu.roll(dense[24 * third:24 * third + 24], 32 + 32 * third, 1) for third in range(3)]
    tail = jnp.where(lane < 32, thirds[0], jnp.where(lane < 64, thirds[1], thirds[2]))
    return jnp.concatenate([dense, tail], axis=0)[:, :96]


def weight_grad_kernel(features, occupancy, own, before, after, grad, columns, windows, dense):
    bricks = [cotangent_of(ref) for ref in (before, own, after)]
    build_windows(bricks, 1, returned_scales(own, before, after), columns, windows)
    masked = (features[0].astype(jnp.float32) * occupancy[...].astype(jnp.float32)).astype(jnp.bfloat16)
    for dx in range(3):
        product = jnp.dot(masked, span(windows, dx), preferred_element_type=jnp.float32)
        for tap in range(9):
            at = 72 * (26 - (9 * dx + tap))
            dense[at:at + 72] = dense_rows(product[:, tap * LANES:(tap + 1) * LANES])
    dense[27 * 72:] = jnp.zeros((ROWS - 27 * 72, LANES), jnp.float32)
    grad[...] = dense[...].astype(jnp.bfloat16).reshape(grad.shape)


def sum_kernel(parts, copies):
    total = parts[0].astype(jnp.float32)
    for part in range(1, parts.shape[0]):
        total = total + parts[part].astype(jnp.float32)
    for copy in range(copies.shape[0]):
        copies[copy] = total.astype(copies.dtype)


def unpack_kernel(dense, grad):
    rows = dense[...].reshape(ROWS, LANES).astype(jnp.float32)
    for tap in range(27):
        grad[tap] = square_rows(rows[72 * tap:72 * tap + 72])


def outputs_kernel(
    occupancy, weight, own, before, after, output, grad_features, columns, windows, taps,
):
    depth = weight.shape[1]
    occupied = occupancy[...].astype(jnp.float32)
    taps[...] = jnp.zeros_like(taps)
    for tap in range(27):
        taps[tap, :depth, :depth] = weight[tap]

    def finish(rows):
        return (rows.T[:depth] * occupied).astype(jnp.bfloat16)

    bricks = [masked_of(ref) for ref in (before, own, after)]
    build_windows(bricks, 1, read_scales(own), columns, windows)
    total = jnp.zeros((VOXELS, LANES), jnp.float32)
    for dx in range(3):
        kernel = taps[9 * dx:9 * dx + 9].reshape(9 * LANES, LANES)
        total = total + jnp.dot(span(windows, dx), kernel, preferred_element_type=jnp.float32)
    output[0] = finish(total)

    bricks = [cotangent_of(ref) for ref in (before, own, after)]
    build_windows(bricks, 1, returned_scales(own, before, after), columns, windows)
    total = jnp.zeros((VOXELS, LANES), jnp.float32)
    for dx in range(3):
        for tap in range(9):
            total = total + lax.dot_general(
                windows[dx:dx + 8, :, tap * LANES:(tap + 1) * LANES].reshape(VOXELS, LANES),
                taps[26 - (9 * dx + tap)],
                (((1,), (1,)), ((), ())),
                preferred_element_type=jnp.float32,
            )
    grad_features[0] = finish(total)


WINDOW_SCRATCH = [
    pltpu.VMEM((3, 10, 10, 8, LANES), jnp.float32),
    pltpu.VMEM((10, 64, 9 * LANES), jnp.bfloat16),
]


def both_ways(block):
    count = lax.axis_size("brick") * lax.axis_size("chan")
    before = lax.ppermute(block, AXES, [(i, i + 1) for i in range(count - 1)])
    after = lax.ppermute(block, AXES, [(i + 1, i) for i in range(count - 1)])
    return before, after


def call(kernel, name, shapes, operands, specs=None, scratch=(), flops=0):
    return pl.pallas_call(
        kernel,
        out_shape=shapes,
        in_specs=specs or [VMEM] * len(operands),
        out_specs=jax.tree.map(lambda _: VMEM, shapes),
        scratch_shapes=list(scratch),
        compiler_params=pltpu.CompilerParams(vmem_limit_bytes=LIMIT),
        cost_estimate=pl.CostEstimate(flops=flops, bytes_accessed=2 * 1024 * 1024, transcendentals=0),
        name=name,
    )(*operands)


def bf16(*shape):
    return jax.ShapeDtypeStruct(shape, jnp.bfloat16)


def total_over_devices(grad):
    rows = grad.shape[1]
    count = NEAR * FAR
    near = [[first + i for i in range(NEAR)] for first in range(0, count, NEAR)]
    far = [[first + NEAR * i for i in range(FAR)] for first in range(NEAR)]
    pieces = lax.all_to_all(grad, AXES, 0, 0, tiled=True, axis_index_groups=near)
    share = call(sum_kernel, "sum_near", bf16(FAR, rows, LANES), (pieces,))
    shares = lax.all_to_all(share, AXES, 0, 0, tiled=True, axis_index_groups=far)
    whole = call(sum_kernel, "sum_far", bf16(NEAR, rows, LANES), (shares,))
    return lax.all_to_all(whole, AXES, 0, 0, tiled=True, axis_index_groups=near)


def shards(features, occupancy, neighbors, weight, grad_output):
    depth = features.shape[1]
    own = call(
        pack_kernel, "pack", bf16(2 * VOXELS + CODES, LANES),
        (neighbors, occupancy, features, grad_output), [SMEM, VMEM, VMEM, VMEM],
    )
    before, after = both_ways(own)
    dot = 27 * 2 * LANES * LANES * VOXELS
    grad = call(
        weight_grad_kernel, "weight_grad", bf16(NEAR, ROWS // NEAR, LANES),
        (features, occupancy, own, before, after),
        scratch=WINDOW_SCRATCH + [pltpu.VMEM((ROWS, LANES), jnp.float32)], flops=dot,
    )
    grad = total_over_devices(grad)
    output, grad_features = call(
        outputs_kernel, "outputs", [bf16(*features.shape)] * 2,
        (occupancy, weight, own, before, after),
        scratch=WINDOW_SCRATCH + [pltpu.VMEM((27, LANES, LANES), jnp.bfloat16)], flops=2 * dot,
    )
    grad_weight = call(unpack_kernel, "unpack", jax.ShapeDtypeStruct((27, depth, depth), jnp.float32), (grad,))
    return output, grad_features, grad_weight


def solution(mesh):
    split = P(AXES, None, None)
    flat = P(AXES, None)
    return jax.shard_map(
        shards,
        mesh=mesh,
        in_specs=(split, flat, flat, P(), split),
        out_specs=(split, split, P()),
        check_vma=False,
    )
```

```python
import jax
import jax.numpy as jnp
from jax import lax
from jax.experimental import pallas as pl
from jax.experimental.pallas import tpu as pltpu
from jax.sharding import PartitionSpec as P

AXES = ("brick", "chan")
SIGNS = (-1, 0, 1)
VOXELS, LANES, CODES = 512, 128, 32
SHELL = 240
ROWS = 2048
NEAR, FAR = 64, 8
FIRST = 4
OWN, MATE, NEXT, NONE = range(4)
HBM = pl.BlockSpec(memory_space=pltpu.HBM)
VMEM = pl.BlockSpec(memory_space=pltpu.VMEM)
SMEM = pl.BlockSpec(memory_space=pltpu.SMEM)
LIMIT = 32 * 1024 * 1024


def voxel_rows(block):
    spare = jnp.zeros((LANES - block.shape[0], block.shape[1]), jnp.float32)
    return jnp.concatenate([block, spare], axis=0).T


def shell_of(brick):
    pieces = [brick[0], brick[7], brick[1:7, 0], brick[1:7, 7], brick[1:7, :, 0], brick[1:7, :, 7]]
    rows = jnp.concatenate([piece.reshape(-1, LANES) for piece in pieces], axis=0)
    tail = jnp.concatenate([pltpu.roll(rows[SHELL:], 96 - 32 * at, 1) for at in range(3)], axis=0)
    lane = lax.broadcasted_iota(jnp.int32, (SHELL, LANES), 1)
    return jnp.where(lane < 96, rows[:SHELL], tail)


def fill_shell(brick, packed):
    third = SHELL // 3
    lane = lax.broadcasted_iota(jnp.int32, (third, LANES), 1)
    thirds = [pltpu.roll(packed[third * at:third * at + third], 32 + 32 * at, 1) for at in range(3)]
    tail = jnp.where(lane < 32, thirds[0], jnp.where(lane < 64, thirds[1], thirds[2]))
    lane = lax.broadcasted_iota(jnp.int32, (SHELL + third, LANES), 1)
    rows = jnp.where(lane < 96, jnp.concatenate([packed, tail], axis=0), 0.0)
    brick[0] = rows[:64].reshape(8, 8, LANES)
    brick[7] = rows[64:128].reshape(8, 8, LANES)
    brick[1:7, 0] = rows[128:176].reshape(6, 8, LANES)
    brick[1:7, 7] = rows[176:224].reshape(6, 8, LANES)
    brick[1:7, 1:7, 0] = rows[224:272].reshape(6, 8, LANES)[:, 1:7]
    brick[1:7, 1:7, 7] = rows[272:].reshape(6, 8, LANES)[:, 1:7]


def pack_kernel(
    neighbors, occupancy, features, grad_output,
    packed, masked, cotangent_rows, masked_rows, table, flags, inputs, brick, arrived,
):
    copies = [
        pltpu.make_async_copy(source, target, arrived.at[at])
        for at, (source, target) in enumerate((
            (occupancy, flags), (grad_output, inputs.at[0:1]), (features, inputs.at[1:2]), (neighbors, table),
        ))
    ]
    for copy in copies:
        copy.start()
    for copy in copies[:2]:
        copy.wait()
    depth = masked.shape[0]
    occupied = flags[...].astype(jnp.float32)
    for at, rows in ((0, cotangent_rows), (1, masked_rows)):
        if at:
            copies[2].wait()
        product = inputs[at].astype(jnp.float32) * occupied
        if at:
            masked[...] = product.astype(jnp.bfloat16)
        by_voxel = voxel_rows(product)
        rows[...] = by_voxel.astype(jnp.bfloat16)
        brick[at] = by_voxel.reshape(8, 8, 8, LANES)
        packed[SHELL * at:SHELL * (at + 1), :] = shell_of(brick.at[at]).astype(jnp.bfloat16)
    copies[3].wait()
    own = table[0, 13]
    mate = own + 1 - 2 * lax.rem(own, 2)
    row = lax.broadcasted_iota(jnp.int32, (CODES, LANES), 0)
    codes = jnp.full((CODES, LANES), NONE, jnp.int32)
    for offset in range(27):
        brick_id = table[0, offset]
        code = jnp.where(brick_id < 0, NONE, jnp.where(brick_id == own, OWN, jnp.where(brick_id == mate, MATE, NEXT)))
        codes = jnp.where(row == offset, code, codes)
    packed[2 * SHELL:, :] = codes.astype(jnp.float32).astype(jnp.bfloat16)


def faces(sign):
    if sign < 0:
        return slice(7, 8), slice(0, 1)
    if sign > 0:
        return slice(0, 1), slice(9, 10)
    return slice(0, 8), slice(1, 9)


def offset_id(x, y, z):
    return 9 * (x + 1) + 3 * (y + 1) + (z + 1)


def build_windows(bricks, weigh, columns, windows):
    for x in SIGNS:
        from_x, to_x = faces(x)
        for y in SIGNS:
            from_y, to_y = faces(y)
            parts = [brick[from_x, from_y] for brick in bricks]
            shape = parts[0].shape

            def side(z):
                return sum(part * scale for part, scale in zip(parts, weigh(x, y, z)))

            middle = parts[OWN] if x == 0 and y == 0 else side(0)
            middle = middle.reshape(-1, 8, LANES)
            below = side(-1).reshape(-1, 8, LANES)
            above = side(1).reshape(-1, 8, LANES)
            row = lax.broadcasted_iota(jnp.int32, middle.shape, 1)
            columns[0, to_x, to_y] = pltpu.roll(jnp.where(row == 7, below, middle), 1, 1).reshape(shape)
            columns[1, to_x, to_y] = middle.reshape(shape)
            columns[2, to_x, to_y] = pltpu.roll(jnp.where(row == 0, above, middle), 7, 1).reshape(shape)
    for dy in range(3):
        for dz in range(3):
            tap = 3 * dy + dz
            for px in range(10):
                windows[px, :, tap * LANES:(tap + 1) * LANES] = (
                    columns[dz, px, dy:dy + 8].reshape(64, LANES).astype(jnp.bfloat16)
                )


def bricks_of(own, mate, beyond, first, shells):
    shells[...] = jnp.zeros_like(shells)
    for at, ref in enumerate((mate, beyond)):
        fill_shell(shells.at[at], ref[first:first + SHELL, :].astype(jnp.float32))
    return [own[...].astype(jnp.float32).reshape(8, 8, 8, LANES), shells[0], shells[1]]


def codes_of(ref):
    return ref[2 * SHELL:, :].astype(jnp.float32)


def returned_scales(own, mate, beyond):
    tables = [codes_of(ref) for ref in (own, mate, beyond)]

    def weigh(x, y, z):
        at = offset_id(-x, -y, -z)
        return [jnp.where(table[at:at + 1] == code, 1.0, 0.0) for code, table in enumerate(tables)]

    return weigh


def read_scales(own):
    table = codes_of(own)

    def weigh(x, y, z):
        at = offset_id(x, y, z)
        return [jnp.where(table[at:at + 1] == code, 1.0, 0.0) for code in (OWN, MATE, NEXT)]

    return weigh


def span(windows, dx):
    return windows[dx:dx + 8].reshape(VOXELS, 9 * LANES)


def dense_rows(block):
    lane = lax.broadcasted_iota(jnp.int32, (72, LANES), 1)
    tail = jnp.concatenate([pltpu.roll(block[72:], 96 - 32 * third, 1) for third in range(3)], axis=0)
    return jnp.where(lane < 96, block[:72], tail)


def square_rows(dense):
    lane = lax.broadcasted_iota(jnp.int32, (24, LANES), 1)
    thirds = [pltpu.roll(dense[24 * third:24 * third + 24], 32 + 32 * third, 1) for third in range(3)]
    tail = jnp.where(lane < 32, thirds[0], jnp.where(lane < 64, thirds[1], thirds[2]))
    return jnp.concatenate([dense, tail], axis=0)[:, :96]


def weight_grad_kernel(masked, own, mate, beyond, cotangent, grad, columns, windows, shells, dense):
    bricks = bricks_of(cotangent, mate, beyond, 0, shells)
    build_windows(bricks, returned_scales(own, mate, beyond), columns, windows)
    for dx in range(3):
        product = jnp.dot(masked[...], span(windows, dx), preferred_element_type=jnp.float32)
        for tap in range(9):
            at = 72 * (26 - (9 * dx + tap))
            dense[at:at + 72] = dense_rows(product[:, tap * LANES:(tap + 1) * LANES])
    dense[27 * 72:] = jnp.zeros((ROWS - 27 * 72, LANES), jnp.float32)
    grad[...] = dense[...].astype(jnp.bfloat16).reshape(grad.shape)


def sum_kernel(parts, copies):
    total = parts[0].astype(jnp.float32)
    for part in range(1, parts.shape[0]):
        total = total + parts[part].astype(jnp.float32)
    for copy in range(copies.shape[0]):
        copies[copy] = total.astype(copies.dtype)


def unpack_kernel(dense, grad):
    rows = dense[...].reshape(ROWS, LANES).astype(jnp.float32)
    for tap in range(27):
        grad[tap] = square_rows(rows[72 * tap:72 * tap + 72])


def outputs_kernel(
    occupancy, weight, own, mate, beyond, cotangent, masked,
    output, grad_features, columns, windows, shells, taps,
):
    depth = weight.shape[1]
    occupied = occupancy[...].astype(jnp.float32)
    taps[...] = jnp.zeros_like(taps)
    for tap in range(27):
        taps[tap, :depth, :depth] = weight[tap]

    def finish(rows):
        return (rows.T[:depth] * occupied).astype(jnp.bfloat16)

    bricks = bricks_of(masked, mate, beyond, SHELL, shells)
    build_windows(bricks, read_scales(own), columns, windows)
    total = jnp.zeros((VOXELS, LANES), jnp.float32)
    for dx in range(3):
        kernel = taps[9 * dx:9 * dx + 9].reshape(9 * LANES, LANES)
        total = total + jnp.dot(span(windows, dx), kernel, preferred_element_type=jnp.float32)
    output[0] = finish(total)

    bricks = bricks_of(cotangent, mate, beyond, 0, shells)
    build_windows(bricks, returned_scales(own, mate, beyond), columns, windows)
    total = jnp.zeros((VOXELS, LANES), jnp.float32)
    for dx in range(3):
        for tap in range(9):
            total = total + lax.dot_general(
                windows[dx:dx + 8, :, tap * LANES:(tap + 1) * LANES].reshape(VOXELS, LANES),
                taps[26 - (9 * dx + tap)],
                (((1,), (1,)), ((), ())),
                preferred_element_type=jnp.float32,
            )
    grad_features[0] = finish(total)


WINDOW_SCRATCH = [
    pltpu.VMEM((3, 10, 10, 8, LANES), jnp.float32),
    pltpu.VMEM((10, 64, 9 * LANES), jnp.bfloat16),
    pltpu.VMEM((2, 8, 8, 8, LANES), jnp.float32),
]


def neighbours(block):
    count = lax.axis_size("brick") * lax.axis_size("chan")
    beyond = lax.ppermute(block, AXES, [(i, i + 2 * (i % 2) - 1) for i in range(1, count - 1)])
    mate = lax.ppermute(block, AXES, [(i, i + 1 - 2 * (i % 2)) for i in range(count)])
    return mate, beyond


def call(kernel, name, shapes, operands, specs=None, scratch=(), flops=0, limit=LIMIT):
    return pl.pallas_call(
        kernel,
        out_shape=shapes,
        in_specs=specs or [VMEM] * len(operands),
        out_specs=jax.tree.map(lambda _: VMEM, shapes),
        scratch_shapes=list(scratch),
        compiler_params=pltpu.CompilerParams(vmem_limit_bytes=limit),
        cost_estimate=pl.CostEstimate(flops=flops, bytes_accessed=2 * 1024 * 1024, transcendentals=0),
        name=name,
    )(*operands)


def bf16(*shape):
    return jax.ShapeDtypeStruct(shape, jnp.bfloat16)


def total_over_devices(grad):
    rows = grad.shape[1]
    count = NEAR * FAR
    near = [[first + i for i in range(NEAR)] for first in range(0, count, NEAR)]
    far = [[first + NEAR * ((i + FIRST) % FAR) for i in range(FAR)] for first in range(NEAR)]
    pieces = lax.all_to_all(grad, AXES, 0, 0, tiled=True, axis_index_groups=near)
    share = call(sum_kernel, "sum_near", bf16(FAR, rows, LANES), (pieces,))
    shares = lax.all_to_all(share, AXES, 0, 0, tiled=True, axis_index_groups=far)
    whole = call(sum_kernel, "sum_far", bf16(NEAR, rows, LANES), (shares,))
    return lax.all_to_all(whole, AXES, 0, 0, tiled=True, axis_index_groups=near)


def shards(features, occupancy, neighbors, weight, grad_output):
    depth = features.shape[1]
    own, masked, cotangent_rows, masked_rows = call(
        pack_kernel, "pack",
        [bf16(2 * SHELL + CODES, LANES), bf16(depth, VOXELS), bf16(VOXELS, LANES), bf16(VOXELS, LANES)],
        (neighbors, occupancy, features, grad_output), [HBM] * 4,
        scratch=[
            pltpu.SMEM(neighbors.shape, jnp.int32),
            pltpu.VMEM(occupancy.shape, jnp.int32),
            pltpu.VMEM((2, depth, VOXELS), jnp.bfloat16),
            pltpu.VMEM((2, 8, 8, 8, LANES), jnp.float32),
            pltpu.SemaphoreType.DMA((4,)),
        ],
    )
    mate, beyond = neighbours(own)
    dot = 27 * 2 * LANES * LANES * VOXELS
    grad = call(
        weight_grad_kernel, "weight_grad", bf16(NEAR, ROWS // NEAR, LANES),
        (masked, own, mate, beyond, cotangent_rows),
        scratch=WINDOW_SCRATCH + [pltpu.VMEM((ROWS, LANES), jnp.float32)], flops=dot,
    )
    grad = total_over_devices(grad)
    output, grad_features = call(
        outputs_kernel, "outputs", [bf16(*features.shape)] * 2,
        (occupancy, weight, own, mate, beyond, cotangent_rows, masked_rows),
        scratch=WINDOW_SCRATCH + [pltpu.VMEM((27, LANES, LANES), jnp.bfloat16)], flops=2 * dot,
    )
    grad_weight = call(unpack_kernel, "unpack", jax.ShapeDtypeStruct((27, depth, depth), jnp.float32), (grad,))
    return output, grad_features, grad_weight


def solution(mesh):
    split = P(AXES, None, None)
    flat = P(AXES, None)
    return jax.shard_map(
        shards,
        mesh=mesh,
        in_specs=(split, flat, flat, P(), split),
        out_specs=(split, split, P()),
        check_vma=False,
    )
```

```python
import jax
import jax.numpy as jnp
from jax import lax
from jax.experimental import pallas as pl
from jax.experimental.pallas import tpu as pltpu
from jax.sharding import PartitionSpec as P

AXES = ("brick", "chan")
SIGNS = (-1, 0, 1)
VOXELS, LANES, CODES = 512, 128, 32
SHELL = 240
ROWS = 2048
NEAR, FAR = 64, 8
SCATTER = [(13 * i + 63) % NEAR for i in range(NEAR)]
GATHER = SCATTER
FIRST = 4
OWN, MATE, NEXT, NONE = range(4)
VMEM = pl.BlockSpec(memory_space=pltpu.VMEM)
LIMIT = 32 * 1024 * 1024


def voxel_rows(block):
    spare = jnp.zeros((LANES - block.shape[0], block.shape[1]), jnp.float32)
    return jnp.concatenate([block, spare], axis=0).T


def shell_of(brick):
    pieces = [brick[0], brick[7], brick[1:7, 0], brick[1:7, 7], brick[1:7, :, 0], brick[1:7, :, 7]]
    rows = jnp.concatenate([piece.reshape(-1, LANES) for piece in pieces], axis=0)
    tail = jnp.concatenate([pltpu.roll(rows[SHELL:], 96 - 32 * at, 1) for at in range(3)], axis=0)
    lane = lax.broadcasted_iota(jnp.int32, (SHELL, LANES), 1)
    return jnp.where(lane < 96, rows[:SHELL], tail)


def fill_shell(brick, packed):
    third = SHELL // 3
    lane = lax.broadcasted_iota(jnp.int32, (third, LANES), 1)
    thirds = [pltpu.roll(packed[third * at:third * at + third], 32 + 32 * at, 1) for at in range(3)]
    tail = jnp.where(lane < 32, thirds[0], jnp.where(lane < 64, thirds[1], thirds[2]))
    lane = lax.broadcasted_iota(jnp.int32, (SHELL + third, LANES), 1)
    rows = jnp.where(lane < 96, jnp.concatenate([packed, tail], axis=0), 0.0)
    brick[0] = rows[:64].reshape(8, 8, LANES)
    brick[7] = rows[64:128].reshape(8, 8, LANES)
    brick[1:7, 0] = rows[128:176].reshape(6, 8, LANES)
    brick[1:7, 7] = rows[176:224].reshape(6, 8, LANES)
    brick[1:7, 1:7, 0] = rows[224:272].reshape(6, 8, LANES)[:, 1:7]
    brick[1:7, 1:7, 7] = rows[272:].reshape(6, 8, LANES)[:, 1:7]


def pack_kernel(pair, side, packed, masked, cotangent_rows, masked_rows, brick):
    occupied = side[0:1, :VOXELS].astype(jnp.float32)
    for at, rows in ((0, cotangent_rows), (1, masked_rows)):
        product = pair[at].astype(jnp.float32) * occupied
        if at:
            masked[...] = product.astype(jnp.bfloat16)
        by_voxel = voxel_rows(product)
        rows[...] = by_voxel.astype(jnp.bfloat16)
        brick[at] = by_voxel.reshape(8, 8, 8, LANES)
        packed[SHELL * at:SHELL * (at + 1), :] = shell_of(brick.at[at]).astype(jnp.bfloat16)
    bricks = side[0:1, VOXELS:VOXELS + LANES]
    lane = lax.broadcasted_iota(jnp.int32, (1, LANES), 1)
    own = jnp.sum(jnp.where(lane == 13, bricks, 0), axis=1, keepdims=True)
    codes = jnp.where(bricks == own, OWN, jnp.where(bricks == (own ^ 1), MATE, NEXT))
    codes = jnp.where(bricks < 0, NONE, codes).astype(jnp.float32)
    packed[2 * SHELL:, :] = jnp.broadcast_to(codes, (LANES, LANES)).T[:CODES].astype(jnp.bfloat16)


def faces(sign):
    if sign < 0:
        return slice(7, 8), slice(0, 1)
    if sign > 0:
        return slice(0, 1), slice(9, 10)
    return slice(0, 8), slice(1, 9)


def offset_id(x, y, z):
    return 9 * (x + 1) + 3 * (y + 1) + (z + 1)


def build_windows(bricks, weigh, columns, windows):
    for x in SIGNS:
        from_x, to_x = faces(x)
        for y in SIGNS:
            from_y, to_y = faces(y)
            parts = [brick[from_x, from_y] for brick in bricks]
            shape = parts[0].shape

            def side(z):
                return sum(part * scale for part, scale in zip(parts, weigh(x, y, z)))

            middle = parts[OWN] if x == 0 and y == 0 else side(0)
            middle = middle.reshape(-1, 8, LANES)
            below = side(-1).reshape(-1, 8, LANES)
            above = side(1).reshape(-1, 8, LANES)
            row = lax.broadcasted_iota(jnp.int32, middle.shape, 1)
            columns[0, to_x, to_y] = pltpu.roll(jnp.where(row == 7, below, middle), 1, 1).reshape(shape)
            columns[1, to_x, to_y] = middle.reshape(shape)
            columns[2, to_x, to_y] = pltpu.roll(jnp.where(row == 0, above, middle), 7, 1).reshape(shape)
    for dy in range(3):
        for dz in range(3):
            tap = 3 * dy + dz
            for px in range(10):
                windows[px, :, tap * LANES:(tap + 1) * LANES] = (
                    columns[dz, px, dy:dy + 8].reshape(64, LANES).astype(jnp.bfloat16)
                )


def bricks_of(own, mate, beyond, first, shells):
    shells[...] = jnp.zeros_like(shells)
    for at, ref in enumerate((mate, beyond)):
        fill_shell(shells.at[at], ref[first:first + SHELL, :].astype(jnp.float32))
    return [own[...].astype(jnp.float32).reshape(8, 8, 8, LANES), shells[0], shells[1]]


def codes_of(ref):
    return ref[2 * SHELL:, :].astype(jnp.float32)


def returned_scales(own, mate, beyond):
    tables = [codes_of(ref) for ref in (own, mate, beyond)]

    def weigh(x, y, z):
        at = offset_id(-x, -y, -z)
        return [jnp.where(table[at:at + 1] == code, 1.0, 0.0) for code, table in enumerate(tables)]

    return weigh


def read_scales(own):
    table = codes_of(own)

    def weigh(x, y, z):
        at = offset_id(x, y, z)
        return [jnp.where(table[at:at + 1] == code, 1.0, 0.0) for code in (OWN, MATE, NEXT)]

    return weigh


def span(windows, dx):
    return windows[dx:dx + 8].reshape(VOXELS, 9 * LANES)


def dense_rows(block):
    lane = lax.broadcasted_iota(jnp.int32, (72, LANES), 1)
    tail = jnp.concatenate([pltpu.roll(block[72:], 96 - 32 * third, 1) for third in range(3)], axis=0)
    return jnp.where(lane < 96, block[:72], tail)


def square_rows(dense):
    lane = lax.broadcasted_iota(jnp.int32, (24, LANES), 1)
    thirds = [pltpu.roll(dense[24 * third:24 * third + 24], 32 + 32 * third, 1) for third in range(3)]
    tail = jnp.where(lane < 32, thirds[0], jnp.where(lane < 64, thirds[1], thirds[2]))
    return jnp.concatenate([dense, tail], axis=0)[:, :96]


def weight_grad_kernel(masked, own, mate, beyond, cotangent, grad, columns, windows, shells, dense):
    bricks = bricks_of(cotangent, mate, beyond, 0, shells)
    build_windows(bricks, returned_scales(own, mate, beyond), columns, windows)
    for dx in range(3):
        product = jnp.dot(masked[...], span(windows, dx), preferred_element_type=jnp.float32)
        for tap in range(9):
            at = 72 * (26 - (9 * dx + tap))
            dense[at:at + 72] = dense_rows(product[:, tap * LANES:(tap + 1) * LANES])
    dense[27 * 72:] = jnp.zeros((ROWS - 27 * 72, LANES), jnp.float32)
    grad[...] = dense[...].astype(jnp.bfloat16).reshape(grad.shape)


def sum_kernel(parts, copies):
    total = parts[0].astype(jnp.float32)
    for part in range(1, parts.shape[0]):
        total = total + parts[part].astype(jnp.float32)
    for copy in range(copies.shape[0]):
        copies[copy] = total.astype(copies.dtype)


def unpack_kernel(dense, grad):
    shares = [dense[GATHER.index(member)] for member in SCATTER]
    rows = jnp.concatenate(shares, axis=0).astype(jnp.float32)
    for tap in range(27):
        grad[tap] = square_rows(rows[72 * tap:72 * tap + 72])


def outputs_kernel(
    occupancy, weight, own, mate, beyond, cotangent, masked,
    output, grad_features, columns, windows, shells, taps,
):
    depth = weight.shape[1]
    occupied = occupancy[...].astype(jnp.float32)
    taps[...] = jnp.zeros_like(taps)
    for tap in range(27):
        taps[tap, :depth, :depth] = weight[tap]

    def finish(rows):
        return (rows.T[:depth] * occupied).astype(jnp.bfloat16)

    bricks = bricks_of(masked, mate, beyond, SHELL, shells)
    build_windows(bricks, read_scales(own), columns, windows)
    total = jnp.zeros((VOXELS, LANES), jnp.float32)
    for dx in range(3):
        kernel = taps[9 * dx:9 * dx + 9].reshape(9 * LANES, LANES)
        total = total + jnp.dot(span(windows, dx), kernel, preferred_element_type=jnp.float32)
    output[0] = finish(total)

    bricks = bricks_of(cotangent, mate, beyond, 0, shells)
    build_windows(bricks, returned_scales(own, mate, beyond), columns, windows)
    total = jnp.zeros((VOXELS, LANES), jnp.float32)
    for dx in range(3):
        for tap in range(9):
            total = total + lax.dot_general(
                windows[dx:dx + 8, :, tap * LANES:(tap + 1) * LANES].reshape(VOXELS, LANES),
                taps[26 - (9 * dx + tap)],
                (((1,), (1,)), ((), ())),
                preferred_element_type=jnp.float32,
            )
    grad_features[0] = finish(total)


WINDOW_SCRATCH = [
    pltpu.VMEM((3, 10, 10, 8, LANES), jnp.float32),
    pltpu.VMEM((10, 64, 9 * LANES), jnp.bfloat16),
    pltpu.VMEM((2, 8, 8, 8, LANES), jnp.float32),
]


def neighbours(block):
    count = lax.axis_size("brick") * lax.axis_size("chan")
    beyond = lax.ppermute(block, AXES, [(i, i + 2 * (i % 2) - 1) for i in range(1, count - 1)])
    mate = lax.ppermute(block, AXES, [(i, i + 1 - 2 * (i % 2)) for i in range(count)])
    return mate, beyond


def call(kernel, name, shapes, operands, specs=None, scratch=(), flops=0, limit=LIMIT):
    return pl.pallas_call(
        kernel,
        out_shape=shapes,
        in_specs=specs or [VMEM] * len(operands),
        out_specs=jax.tree.map(lambda _: VMEM, shapes),
        scratch_shapes=list(scratch),
        compiler_params=pltpu.CompilerParams(vmem_limit_bytes=limit),
        cost_estimate=pl.CostEstimate(flops=flops, bytes_accessed=2 * 1024 * 1024, transcendentals=0),
        name=name,
    )(*operands)


def bf16(*shape):
    return jax.ShapeDtypeStruct(shape, jnp.bfloat16)


def near_groups(order):
    count = NEAR * FAR
    return [[first + member for member in order] for first in range(0, count, NEAR)]


def total_over_devices(grad):
    rows = grad.shape[1]
    far = [[first + NEAR * ((i + FIRST) % FAR) for i in range(FAR)] for first in range(NEAR)]
    pieces = lax.all_to_all(grad, AXES, 0, 0, tiled=True, axis_index_groups=near_groups(SCATTER))
    share = call(sum_kernel, "sum_near", bf16(FAR, rows, LANES), (pieces,))
    shares = lax.all_to_all(share, AXES, 0, 0, tiled=True, axis_index_groups=far)
    whole = call(sum_kernel, "sum_far", bf16(NEAR, rows, LANES), (shares,))
    return lax.all_to_all(whole, AXES, 0, 0, tiled=True, axis_index_groups=near_groups(GATHER))


def shards(features, occupancy, neighbors, weight, grad_output):
    depth = features.shape[1]
    pair = jnp.concatenate([grad_output, features])
    side = jnp.pad(neighbors, ((0, 0), (VOXELS, LANES - 27))) + jnp.pad(occupancy, ((0, 0), (0, LANES)))
    own, masked, cotangent_rows, masked_rows = call(
        pack_kernel, "pack",
        [bf16(2 * SHELL + CODES, LANES), bf16(depth, VOXELS), bf16(VOXELS, LANES), bf16(VOXELS, LANES)],
        (pair, side), scratch=[pltpu.VMEM((2, 8, 8, 8, LANES), jnp.float32)],
    )
    mate, beyond = neighbours(own)
    dot = 27 * 2 * LANES * LANES * VOXELS
    grad = call(
        weight_grad_kernel, "weight_grad", bf16(NEAR, ROWS // NEAR, LANES),
        (masked, own, mate, beyond, cotangent_rows),
        scratch=WINDOW_SCRATCH + [pltpu.VMEM((ROWS, LANES), jnp.float32)], flops=dot,
    )
    grad = total_over_devices(grad)
    output, grad_features = call(
        outputs_kernel, "outputs", [bf16(*features.shape)] * 2,
        (occupancy, weight, own, mate, beyond, cotangent_rows, masked_rows),
        scratch=WINDOW_SCRATCH + [pltpu.VMEM((27, LANES, LANES), jnp.bfloat16)], flops=2 * dot,
    )
    grad_weight = call(unpack_kernel, "unpack", jax.ShapeDtypeStruct((27, depth, depth), jnp.float32), (grad,))
    return output, grad_features, grad_weight


def solution(mesh):
    split = P(AXES, None, None)
    flat = P(AXES, None)
    return jax.shard_map(
        shards,
        mesh=mesh,
        in_specs=(split, flat, flat, P(), split),
        out_specs=(split, split, P()),
        check_vma=False,
    )
```

```python
import jax
import jax.numpy as jnp
from jax import lax
from jax.experimental import pallas as pl
from jax.experimental.pallas import tpu as pltpu
from jax.sharding import PartitionSpec as P

AXES = ("brick", "chan")
SIGNS = (-1, 0, 1)
VOXELS, LANES, CODES = 512, 128, 32
STACK = 200
SHELL = 240
ROWS = 2048
NEAR, FAR = 64, 8


def crossing(stride):
    chips = [(stride * j + 31) % 32 for j in range(32)]
    return [member for j in range(32) for member in (2 * chips[j] + 1, 2 * chips[-j])]


SCATTER = crossing(13)
GATHER = crossing(1)
FIRST = 4
OWN, MATE, NEXT, NONE = range(4)
VMEM = pl.BlockSpec(memory_space=pltpu.VMEM)
LIMIT = 32 * 1024 * 1024


def voxel_rows(block):
    spare = jnp.zeros((LANES - block.shape[0], block.shape[1]), jnp.float32)
    return jnp.concatenate([block, spare], axis=0).T


def shell_of(brick):
    pieces = [brick[0], brick[7], brick[1:7, 0], brick[1:7, 7], brick[1:7, :, 0], brick[1:7, :, 7]]
    rows = jnp.concatenate([piece.reshape(-1, LANES) for piece in pieces], axis=0)
    tail = jnp.concatenate([pltpu.roll(rows[SHELL:], 96 - 32 * at, 1) for at in range(3)], axis=0)
    lane = lax.broadcasted_iota(jnp.int32, (SHELL, LANES), 1)
    return jnp.where(lane < 96, rows[:SHELL], tail)


def fill_shell(brick, packed):
    third = SHELL // 3
    lane = lax.broadcasted_iota(jnp.int32, (third, LANES), 1)
    thirds = [pltpu.roll(packed[third * at:third * at + third], 32 + 32 * at, 1) for at in range(3)]
    tail = jnp.where(lane < 32, thirds[0], jnp.where(lane < 64, thirds[1], thirds[2]))
    lane = lax.broadcasted_iota(jnp.int32, (SHELL + third, LANES), 1)
    rows = jnp.where(lane < 96, jnp.concatenate([packed, tail], axis=0), 0.0)
    brick[0] = rows[:64].reshape(8, 8, LANES)
    brick[7] = rows[64:128].reshape(8, 8, LANES)
    brick[1:7, 0] = rows[128:176].reshape(6, 8, LANES)
    brick[1:7, 7] = rows[176:224].reshape(6, 8, LANES)
    brick[1:7, 1:7, 0] = rows[224:272].reshape(6, 8, LANES)[:, 1:7]
    brick[1:7, 1:7, 7] = rows[272:].reshape(6, 8, LANES)[:, 1:7]


def stacked(features, occupancy, neighbors, grad_output):
    depth = features.shape[0]

    def rows(block, first):
        return jnp.pad(block, ((first, STACK - first - block.shape[0]), (0, VOXELS - block.shape[1]))).astype(jnp.float32)

    return (
        rows(grad_output, 0) + rows(features, depth) + rows(occupancy, 2 * depth) + rows(neighbors, 2 * depth + 1)
    )


def pack_kernel(stack, packed, masked, cotangent_rows, masked_rows, brick):
    depth = masked.shape[0]
    side = stack[2 * depth:, :]
    occupied = side[0:1]
    for at, rows in ((0, cotangent_rows), (1, masked_rows)):
        product = stack[depth * at:depth * (at + 1), :] * occupied
        if at:
            masked[...] = product.astype(jnp.bfloat16)
        by_voxel = voxel_rows(product)
        rows[...] = by_voxel.astype(jnp.bfloat16)
        brick[at] = by_voxel.reshape(8, 8, 8, LANES)
        packed[SHELL * at:SHELL * (at + 1), :] = shell_of(brick.at[at]).astype(jnp.bfloat16)
    bricks = side[1:2, :LANES].astype(jnp.int32)
    lane = lax.broadcasted_iota(jnp.int32, (1, LANES), 1)
    own = jnp.sum(jnp.where(lane == 13, bricks, 0), axis=1, keepdims=True)
    codes = jnp.where(bricks == own, OWN, jnp.where(bricks == (own ^ 1), MATE, NEXT))
    codes = jnp.where(bricks < 0, NONE, codes).astype(jnp.float32)
    packed[2 * SHELL:, :] = jnp.broadcast_to(codes, (LANES, LANES)).T[:CODES].astype(jnp.bfloat16)


def faces(sign):
    if sign < 0:
        return slice(7, 8), slice(0, 1)
    if sign > 0:
        return slice(0, 1), slice(9, 10)
    return slice(0, 8), slice(1, 9)


def offset_id(x, y, z):
    return 9 * (x + 1) + 3 * (y + 1) + (z + 1)


def build_windows(bricks, weigh, columns, windows):
    for x in SIGNS:
        from_x, to_x = faces(x)
        for y in SIGNS:
            from_y, to_y = faces(y)
            parts = [brick[from_x, from_y] for brick in bricks]
            shape = parts[0].shape

            def side(z):
                return sum(part * scale for part, scale in zip(parts, weigh(x, y, z)))

            middle = parts[OWN] if x == 0 and y == 0 else side(0)
            middle = middle.reshape(-1, 8, LANES)
            below = side(-1).reshape(-1, 8, LANES)
            above = side(1).reshape(-1, 8, LANES)
            row = lax.broadcasted_iota(jnp.int32, middle.shape, 1)
            columns[0, to_x, to_y] = pltpu.roll(jnp.where(row == 7, below, middle), 1, 1).reshape(shape)
            columns[1, to_x, to_y] = middle.reshape(shape)
            columns[2, to_x, to_y] = pltpu.roll(jnp.where(row == 0, above, middle), 7, 1).reshape(shape)
    for dy in range(3):
        for dz in range(3):
            tap = 3 * dy + dz
            for px in range(10):
                windows[px, :, tap * LANES:(tap + 1) * LANES] = (
                    columns[dz, px, dy:dy + 8].reshape(64, LANES).astype(jnp.bfloat16)
                )


def bricks_of(own, mate, beyond, first, shells):
    shells[...] = jnp.zeros_like(shells)
    for at, ref in enumerate((mate, beyond)):
        fill_shell(shells.at[at], ref[first:first + SHELL, :].astype(jnp.float32))
    return [own[...].astype(jnp.float32).reshape(8, 8, 8, LANES), shells[0], shells[1]]


def codes_of(ref):
    return ref[2 * SHELL:, :].astype(jnp.float32)


def returned_scales(own, mate, beyond):
    tables = [codes_of(ref) for ref in (own, mate, beyond)]

    def weigh(x, y, z):
        at = offset_id(-x, -y, -z)
        return [jnp.where(table[at:at + 1] == code, 1.0, 0.0) for code, table in enumerate(tables)]

    return weigh


def read_scales(own):
    table = codes_of(own)

    def weigh(x, y, z):
        at = offset_id(x, y, z)
        return [jnp.where(table[at:at + 1] == code, 1.0, 0.0) for code in (OWN, MATE, NEXT)]

    return weigh


def span(windows, dx):
    return windows[dx:dx + 8].reshape(VOXELS, 9 * LANES)


def dense_rows(block):
    lane = lax.broadcasted_iota(jnp.int32, (72, LANES), 1)
    tail = jnp.concatenate([pltpu.roll(block[72:], 96 - 32 * third, 1) for third in range(3)], axis=0)
    return jnp.where(lane < 96, block[:72], tail)


def square_rows(dense):
    lane = lax.broadcasted_iota(jnp.int32, (24, LANES), 1)
    thirds = [pltpu.roll(dense[24 * third:24 * third + 24], 32 + 32 * third, 1) for third in range(3)]
    tail = jnp.where(lane < 32, thirds[0], jnp.where(lane < 64, thirds[1], thirds[2]))
    return jnp.concatenate([dense, tail], axis=0)[:, :96]


def weight_grad_kernel(masked, own, mate, beyond, cotangent, grad, columns, windows, shells, dense):
    bricks = bricks_of(cotangent, mate, beyond, 0, shells)
    build_windows(bricks, returned_scales(own, mate, beyond), columns, windows)
    for dx in range(3):
        product = jnp.dot(masked[...], span(windows, dx), preferred_element_type=jnp.float32)
        for tap in range(9):
            at = 72 * (26 - (9 * dx + tap))
            dense[at:at + 72] = dense_rows(product[:, tap * LANES:(tap + 1) * LANES])
    dense[27 * 72:] = jnp.zeros((ROWS - 27 * 72, LANES), jnp.float32)
    grad[...] = dense[...].astype(jnp.bfloat16).reshape(grad.shape)


def sum_kernel(parts, copies):
    total = parts[0].astype(jnp.float32)
    for part in range(1, parts.shape[0]):
        total = total + parts[part].astype(jnp.float32)
    for copy in range(copies.shape[0]):
        copies[copy] = total.astype(copies.dtype)


def unpack_kernel(dense, grad):
    shares = [dense[GATHER.index(member)] for member in SCATTER]
    rows = jnp.concatenate(shares, axis=0).astype(jnp.float32)
    for tap in range(27):
        grad[tap] = square_rows(rows[72 * tap:72 * tap + 72])


def outputs_kernel(
    occupancy, weight, own, mate, beyond, cotangent, masked,
    output, grad_features, columns, windows, shells, taps,
):
    depth = weight.shape[1]
    occupied = occupancy[...].astype(jnp.float32)
    taps[...] = jnp.zeros_like(taps)
    for tap in range(27):
        taps[tap, :depth, :depth] = weight[tap]

    def finish(rows):
        return (rows.T[:depth] * occupied).astype(jnp.bfloat16)

    bricks = bricks_of(masked, mate, beyond, SHELL, shells)
    build_windows(bricks, read_scales(own), columns, windows)
    total = jnp.zeros((VOXELS, LANES), jnp.float32)
    for dx in range(3):
        kernel = taps[9 * dx:9 * dx + 9].reshape(9 * LANES, LANES)
        total = total + jnp.dot(span(windows, dx), kernel, preferred_element_type=jnp.float32)
    output[0] = finish(total)

    bricks = bricks_of(cotangent, mate, beyond, 0, shells)
    build_windows(bricks, returned_scales(own, mate, beyond), columns, windows)
    total = jnp.zeros((VOXELS, LANES), jnp.float32)
    for dx in range(3):
        for tap in range(9):
            total = total + lax.dot_general(
                windows[dx:dx + 8, :, tap * LANES:(tap + 1) * LANES].reshape(VOXELS, LANES),
                taps[26 - (9 * dx + tap)],
                (((1,), (1,)), ((), ())),
                preferred_element_type=jnp.float32,
            )
    grad_features[0] = finish(total)


WINDOW_SCRATCH = [
    pltpu.VMEM((3, 10, 10, 8, LANES), jnp.float32),
    pltpu.VMEM((10, 64, 9 * LANES), jnp.bfloat16),
    pltpu.VMEM((2, 8, 8, 8, LANES), jnp.float32),
]


def neighbours(block):
    count = lax.axis_size("brick") * lax.axis_size("chan")
    beyond = lax.ppermute(block, AXES, [(i, i + 2 * (i % 2) - 1) for i in range(1, count - 1)])
    mate = lax.ppermute(block, AXES, [(i, i + 1 - 2 * (i % 2)) for i in range(count)])
    return mate, beyond


def call(kernel, name, shapes, operands, specs=None, scratch=(), flops=0, limit=LIMIT):
    return pl.pallas_call(
        kernel,
        out_shape=shapes,
        in_specs=specs or [VMEM] * len(operands),
        out_specs=jax.tree.map(lambda _: VMEM, shapes),
        scratch_shapes=list(scratch),
        compiler_params=pltpu.CompilerParams(vmem_limit_bytes=limit),
        cost_estimate=pl.CostEstimate(flops=flops, bytes_accessed=2 * 1024 * 1024, transcendentals=0),
        name=name,
    )(*operands)


def bf16(*shape):
    return jax.ShapeDtypeStruct(shape, jnp.bfloat16)


def near_groups(order):
    count = NEAR * FAR
    return [[first + member for member in order] for first in range(0, count, NEAR)]


def total_over_devices(grad):
    rows = grad.shape[1]
    far = [[first + NEAR * ((i + FIRST) % FAR) for i in range(FAR)] for first in range(NEAR)]
    pieces = lax.all_to_all(grad, AXES, 0, 0, tiled=True, axis_index_groups=near_groups(SCATTER))
    share = call(sum_kernel, "sum_near", bf16(FAR, rows, LANES), (pieces,))
    shares = lax.all_to_all(share, AXES, 0, 0, tiled=True, axis_index_groups=far)
    whole = call(sum_kernel, "sum_far", bf16(NEAR, rows, LANES), (shares,))
    return lax.all_to_all(whole, AXES, 0, 0, tiled=True, axis_index_groups=near_groups(GATHER))


def shards(features, occupancy, neighbors, weight, grad_output):
    depth = features.shape[1]
    stack = stacked(features[0], occupancy, neighbors, grad_output[0])
    own, masked, cotangent_rows, masked_rows = call(
        pack_kernel, "pack",
        [bf16(2 * SHELL + CODES, LANES), bf16(depth, VOXELS), bf16(VOXELS, LANES), bf16(VOXELS, LANES)],
        (stack,), scratch=[pltpu.VMEM((2, 8, 8, 8, LANES), jnp.float32)],
    )
    mate, beyond = neighbours(own)
    dot = 27 * 2 * LANES * LANES * VOXELS
    grad = call(
        weight_grad_kernel, "weight_grad", bf16(NEAR, ROWS // NEAR, LANES),
        (masked, own, mate, beyond, cotangent_rows),
        scratch=WINDOW_SCRATCH + [pltpu.VMEM((ROWS, LANES), jnp.float32)], flops=dot,
    )
    grad = total_over_devices(grad)
    output, grad_features = call(
        outputs_kernel, "outputs", [bf16(*features.shape)] * 2,
        (occupancy, weight, own, mate, beyond, cotangent_rows, masked_rows),
        scratch=WINDOW_SCRATCH + [pltpu.VMEM((27, LANES, LANES), jnp.bfloat16)], flops=2 * dot,
    )
    grad_weight = call(unpack_kernel, "unpack", jax.ShapeDtypeStruct((27, depth, depth), jnp.float32), (grad,))
    return output, grad_features, grad_weight


def solution(mesh):
    split = P(AXES, None, None)
    flat = P(AXES, None)
    return jax.shard_map(
        shards,
        mesh=mesh,
        in_specs=(split, flat, flat, P(), split),
        out_specs=(split, split, P()),
        check_vma=False,
    )
```

```python
import jax
import jax.numpy as jnp
from jax import lax
from jax.experimental import pallas as pl
from jax.experimental.pallas import tpu as pltpu
from jax.sharding import PartitionSpec as P

AXES = ("brick", "chan")
SIGNS = (-1, 0, 1)
VOXELS, LANES, CODES = 512, 128, 32
STACK = 200
SHELL = 240
ROWS = 2048
NEAR, FAR = 64, 8


def crossing(stride):
    chips = [(stride * j + 31) % 32 for j in range(32)]
    return [member for j in range(32) for member in (2 * chips[j] + 1, 2 * chips[-j])]


SCATTER = crossing(11)
GATHER = crossing(11)
FIRST = 4
OWN, MATE, NEXT, NONE = range(4)
VMEM = pl.BlockSpec(memory_space=pltpu.VMEM)
LIMIT = 32 * 1024 * 1024


def voxel_rows(block):
    spare = jnp.zeros((LANES - block.shape[0], block.shape[1]), jnp.float32)
    return jnp.concatenate([block, spare], axis=0).T


def shell_of(brick):
    pieces = [brick[0], brick[7], brick[1:7, 0], brick[1:7, 7], brick[1:7, :, 0], brick[1:7, :, 7]]
    rows = jnp.concatenate([piece.reshape(-1, LANES) for piece in pieces], axis=0)
    tail = jnp.concatenate([pltpu.roll(rows[SHELL:], 96 - 32 * at, 1) for at in range(3)], axis=0)
    lane = lax.broadcasted_iota(jnp.int32, (SHELL, LANES), 1)
    return jnp.where(lane < 96, rows[:SHELL], tail)


def fill_shell(brick, packed):
    third = SHELL // 3
    lane = lax.broadcasted_iota(jnp.int32, (third, LANES), 1)
    thirds = [pltpu.roll(packed[third * at:third * at + third], 32 + 32 * at, 1) for at in range(3)]
    tail = jnp.where(lane < 32, thirds[0], jnp.where(lane < 64, thirds[1], thirds[2]))
    lane = lax.broadcasted_iota(jnp.int32, (SHELL + third, LANES), 1)
    rows = jnp.where(lane < 96, jnp.concatenate([packed, tail], axis=0), 0.0)
    brick[0] = rows[:64].reshape(8, 8, LANES)
    brick[7] = rows[64:128].reshape(8, 8, LANES)
    brick[1:7, 0] = rows[128:176].reshape(6, 8, LANES)
    brick[1:7, 7] = rows[176:224].reshape(6, 8, LANES)
    brick[1:7, 1:7, 0] = rows[224:272].reshape(6, 8, LANES)[:, 1:7]
    brick[1:7, 1:7, 7] = rows[272:].reshape(6, 8, LANES)[:, 1:7]


def stacked(features, occupancy, neighbors, grad_output):
    depth = features.shape[0]

    def rows(block, first):
        return jnp.pad(block, ((first, STACK - first - block.shape[0]), (0, VOXELS - block.shape[1]))).astype(jnp.float32)

    return (
        rows(grad_output, 0) + rows(features, depth) + rows(occupancy, 2 * depth) + rows(neighbors, 2 * depth + 1)
    )


def pack_kernel(stack, packed, masked, cotangent_rows, masked_rows, brick):
    depth = masked.shape[0]
    side = stack[2 * depth:, :]
    occupied = side[0:1]
    for at, rows in ((0, cotangent_rows), (1, masked_rows)):
        product = stack[depth * at:depth * (at + 1), :] * occupied
        if at:
            masked[...] = product.astype(jnp.bfloat16)
        by_voxel = voxel_rows(product)
        rows[...] = by_voxel.astype(jnp.bfloat16)
        brick[at] = by_voxel.reshape(8, 8, 8, LANES)
        packed[SHELL * at:SHELL * (at + 1), :] = shell_of(brick.at[at]).astype(jnp.bfloat16)
    bricks = side[1:2, :LANES].astype(jnp.int32)
    lane = lax.broadcasted_iota(jnp.int32, (1, LANES), 1)
    own = jnp.sum(jnp.where(lane == 13, bricks, 0), axis=1, keepdims=True)
    codes = jnp.where(bricks == own, OWN, jnp.where(bricks == (own ^ 1), MATE, NEXT))
    codes = jnp.where(bricks < 0, NONE, codes).astype(jnp.float32)
    packed[2 * SHELL:, :] = jnp.broadcast_to(codes, (LANES, LANES)).T[:CODES].astype(jnp.bfloat16)


def faces(sign):
    if sign < 0:
        return slice(7, 8), slice(0, 1)
    if sign > 0:
        return slice(0, 1), slice(9, 10)
    return slice(0, 8), slice(1, 9)


def offset_id(x, y, z):
    return 9 * (x + 1) + 3 * (y + 1) + (z + 1)


def build_windows(bricks, weigh, columns, windows):
    for x in SIGNS:
        from_x, to_x = faces(x)
        for y in SIGNS:
            from_y, to_y = faces(y)
            parts = [brick[from_x, from_y] for brick in bricks]
            shape = parts[0].shape

            def side(z):
                return sum(part * scale for part, scale in zip(parts, weigh(x, y, z)))

            middle = parts[OWN] if x == 0 and y == 0 else side(0)
            middle = middle.reshape(-1, 8, LANES)
            below = side(-1).reshape(-1, 8, LANES)
            above = side(1).reshape(-1, 8, LANES)
            row = lax.broadcasted_iota(jnp.int32, middle.shape, 1)
            columns[0, to_x, to_y] = pltpu.roll(jnp.where(row == 7, below, middle), 1, 1).reshape(shape)
            columns[1, to_x, to_y] = middle.reshape(shape)
            columns[2, to_x, to_y] = pltpu.roll(jnp.where(row == 0, above, middle), 7, 1).reshape(shape)
    for dy in range(3):
        for dz in range(3):
            tap = 3 * dy + dz
            for px in range(10):
                windows[px, :, tap * LANES:(tap + 1) * LANES] = (
                    columns[dz, px, dy:dy + 8].reshape(64, LANES).astype(jnp.bfloat16)
                )


def bricks_of(own, mate, beyond, first, shells):
    shells[...] = jnp.zeros_like(shells)
    for at, ref in enumerate((mate, beyond)):
        fill_shell(shells.at[at], ref[first:first + SHELL, :].astype(jnp.float32))
    return [own[...].astype(jnp.float32).reshape(8, 8, 8, LANES), shells[0], shells[1]]


def codes_of(ref):
    return ref[2 * SHELL:, :].astype(jnp.float32)


def returned_scales(own, mate, beyond):
    tables = [codes_of(ref) for ref in (own, mate, beyond)]

    def weigh(x, y, z):
        at = offset_id(-x, -y, -z)
        return [jnp.where(table[at:at + 1] == code, 1.0, 0.0) for code, table in enumerate(tables)]

    return weigh


def read_scales(own):
    table = codes_of(own)

    def weigh(x, y, z):
        at = offset_id(x, y, z)
        return [jnp.where(table[at:at + 1] == code, 1.0, 0.0) for code in (OWN, MATE, NEXT)]

    return weigh


def span(windows, dx):
    return windows[dx:dx + 8].reshape(VOXELS, 9 * LANES)


def dense_rows(block):
    lane = lax.broadcasted_iota(jnp.int32, (72, LANES), 1)
    tail = jnp.concatenate([pltpu.roll(block[72:], 96 - 32 * third, 1) for third in range(3)], axis=0)
    return jnp.where(lane < 96, block[:72], tail)


def square_rows(dense, square):
    square[:72] = dense[:, :96]
    lane = lax.broadcasted_iota(jnp.int32, (24, LANES), 1)
    thirds = [pltpu.roll(dense[24 * third:24 * third + 24], 32 + 32 * third, 1) for third in range(3)]
    tail = jnp.where(lane < 32, thirds[0], jnp.where(lane < 64, thirds[1], thirds[2]))
    square[72:] = tail[:, :96]


def weight_grad_kernel(masked, own, mate, beyond, cotangent, grad, columns, windows, shells, dense):
    bricks = bricks_of(cotangent, mate, beyond, 0, shells)
    build_windows(bricks, returned_scales(own, mate, beyond), columns, windows)
    for dx in range(3):
        product = jnp.dot(masked[...], span(windows, dx), preferred_element_type=jnp.float32)
        for tap in range(9):
            at = 72 * (26 - (9 * dx + tap))
            dense[at:at + 72] = dense_rows(product[:, tap * LANES:(tap + 1) * LANES])
    dense[27 * 72:] = jnp.zeros((ROWS - 27 * 72, LANES), jnp.float32)
    grad[...] = dense[...].astype(jnp.bfloat16).reshape(grad.shape)


def sum_kernel(parts, copies):
    total = parts[0].astype(jnp.float32)
    for part in range(1, parts.shape[0]):
        total = total + parts[part].astype(jnp.float32)
    for copy in range(copies.shape[0]):
        copies[copy] = total.astype(copies.dtype)


def unpack_kernel(dense, grad):
    shares = [dense[GATHER.index(member)] for member in SCATTER]
    rows = jnp.concatenate(shares, axis=0).astype(jnp.float32)
    for tap in range(27):
        square_rows(rows[72 * tap:72 * tap + 72], grad.at[tap])


def outputs_kernel(
    occupancy, weight, own, mate, beyond, cotangent, masked,
    output, grad_features, columns, windows, shells, taps,
):
    depth = weight.shape[1]
    occupied = occupancy[...].astype(jnp.float32)
    taps[...] = jnp.zeros_like(taps)
    for tap in range(27):
        taps[tap, :depth, :depth] = weight[tap]

    def finish(rows):
        return (rows.T[:depth] * occupied).astype(jnp.bfloat16)

    bricks = bricks_of(masked, mate, beyond, SHELL, shells)
    build_windows(bricks, read_scales(own), columns, windows)
    total = jnp.zeros((VOXELS, LANES), jnp.float32)
    for dx in range(3):
        kernel = taps[9 * dx:9 * dx + 9].reshape(9 * LANES, LANES)
        total = total + jnp.dot(span(windows, dx), kernel, preferred_element_type=jnp.float32)
    output[0] = finish(total)

    bricks = bricks_of(cotangent, mate, beyond, 0, shells)
    build_windows(bricks, returned_scales(own, mate, beyond), columns, windows)
    total = jnp.zeros((VOXELS, LANES), jnp.float32)
    for dx in range(3):
        for tap in range(9):
            total = total + lax.dot_general(
                windows[dx:dx + 8, :, tap * LANES:(tap + 1) * LANES].reshape(VOXELS, LANES),
                taps[26 - (9 * dx + tap)],
                (((1,), (1,)), ((), ())),
                preferred_element_type=jnp.float32,
            )
    grad_features[0] = finish(total)


WINDOW_SCRATCH = [
    pltpu.VMEM((3, 10, 10, 8, LANES), jnp.float32),
    pltpu.VMEM((10, 64, 9 * LANES), jnp.bfloat16),
    pltpu.VMEM((2, 8, 8, 8, LANES), jnp.float32),
]


def neighbours(block):
    count = lax.axis_size("brick") * lax.axis_size("chan")
    beyond = lax.ppermute(block, AXES, [(i, i + 2 * (i % 2) - 1) for i in range(1, count - 1)])
    mate = lax.ppermute(block, AXES, [(i, i + 1 - 2 * (i % 2)) for i in range(count)])
    return mate, beyond


def call(kernel, name, shapes, operands, specs=None, scratch=(), flops=0, limit=LIMIT):
    return pl.pallas_call(
        kernel,
        out_shape=shapes,
        in_specs=specs or [VMEM] * len(operands),
        out_specs=jax.tree.map(lambda _: VMEM, shapes),
        scratch_shapes=list(scratch),
        compiler_params=pltpu.CompilerParams(vmem_limit_bytes=limit),
        cost_estimate=pl.CostEstimate(flops=flops, bytes_accessed=2 * 1024 * 1024, transcendentals=0),
        name=name,
    )(*operands)


def bf16(*shape):
    return jax.ShapeDtypeStruct(shape, jnp.bfloat16)


def near_groups(order):
    count = NEAR * FAR
    return [[first + member for member in order] for first in range(0, count, NEAR)]


def total_over_devices(grad):
    rows = grad.shape[1]
    far = [[first + NEAR * ((i + FIRST) % FAR) for i in range(FAR)] for first in range(NEAR)]
    pieces = lax.all_to_all(grad, AXES, 0, 0, tiled=True, axis_index_groups=near_groups(SCATTER))
    share = call(sum_kernel, "sum_near", bf16(FAR, rows, LANES), (pieces,))
    shares = lax.all_to_all(share, AXES, 0, 0, tiled=True, axis_index_groups=far)
    whole = call(sum_kernel, "sum_far", bf16(NEAR, rows, LANES), (shares,))
    return lax.all_to_all(whole, AXES, 0, 0, tiled=True, axis_index_groups=near_groups(GATHER))


def shards(features, occupancy, neighbors, weight, grad_output):
    depth = features.shape[1]
    stack = stacked(features[0], occupancy, neighbors, grad_output[0])
    own, masked, cotangent_rows, masked_rows = call(
        pack_kernel, "pack",
        [bf16(2 * SHELL + CODES, LANES), bf16(depth, VOXELS), bf16(VOXELS, LANES), bf16(VOXELS, LANES)],
        (stack,), scratch=[pltpu.VMEM((2, 8, 8, 8, LANES), jnp.float32)],
    )
    mate, beyond = neighbours(own)
    dot = 27 * 2 * LANES * LANES * VOXELS
    grad = call(
        weight_grad_kernel, "weight_grad", bf16(NEAR, ROWS // NEAR, LANES),
        (masked, own, mate, beyond, cotangent_rows),
        scratch=WINDOW_SCRATCH + [pltpu.VMEM((ROWS, LANES), jnp.float32)], flops=dot,
    )
    grad = total_over_devices(grad)
    output, grad_features = call(
        outputs_kernel, "outputs", [bf16(*features.shape)] * 2,
        (occupancy, weight, own, mate, beyond, cotangent_rows, masked_rows),
        scratch=WINDOW_SCRATCH + [pltpu.VMEM((27, LANES, LANES), jnp.bfloat16)], flops=2 * dot,
    )
    grad_weight = call(unpack_kernel, "unpack", jax.ShapeDtypeStruct((27, depth, depth), jnp.float32), (grad,))
    return output, grad_features, grad_weight


def solution(mesh):
    split = P(AXES, None, None)
    flat = P(AXES, None)
    return jax.shard_map(
        shards,
        mesh=mesh,
        in_specs=(split, flat, flat, P(), split),
        out_specs=(split, split, P()),
        check_vma=False,
    )
```

```python
import jax
import jax.numpy as jnp
from jax import lax
from jax.experimental import pallas as pl
from jax.experimental.pallas import tpu as pltpu
from jax.sharding import PartitionSpec as P

AXES = ("brick", "chan")
SIGNS = (-1, 0, 1)
VOXELS, LANES, CODES = 512, 128, 32
STACK = 200
SHELL = 240
ROWS = 2048
NEAR, FAR = 64, 8


def crossing(stride, lead):
    chips = [(stride * j + 31) % 32 for j in range(32)]
    return [member for j in range(32) for member in (2 * chips[j] + lead, 2 * chips[-j] + 1 - lead)]


SCATTER = crossing(11, 0)
GATHER = crossing(11, 1)
FIRST = 4
OWN, MATE, NEXT, NONE = range(4)
VMEM = pl.BlockSpec(memory_space=pltpu.VMEM)
LIMIT = 32 * 1024 * 1024


def voxel_rows(block):
    spare = jnp.zeros((LANES - block.shape[0], block.shape[1]), jnp.float32)
    return jnp.concatenate([block, spare], axis=0).T


def shell_of(brick):
    pieces = [brick[0], brick[7], brick[1:7, 0], brick[1:7, 7], brick[1:7, :, 0], brick[1:7, :, 7]]
    rows = jnp.concatenate([piece.reshape(-1, LANES) for piece in pieces], axis=0)
    tail = jnp.concatenate([pltpu.roll(rows[SHELL:], 96 - 32 * at, 1) for at in range(3)], axis=0)
    lane = lax.broadcasted_iota(jnp.int32, (SHELL, LANES), 1)
    return jnp.where(lane < 96, rows[:SHELL], tail)


def fill_shell(brick, packed):
    third = SHELL // 3
    lane = lax.broadcasted_iota(jnp.int32, (third, LANES), 1)
    thirds = [pltpu.roll(packed[third * at:third * at + third], 32 + 32 * at, 1) for at in range(3)]
    tail = jnp.where(lane < 32, thirds[0], jnp.where(lane < 64, thirds[1], thirds[2]))
    lane = lax.broadcasted_iota(jnp.int32, (SHELL + third, LANES), 1)
    rows = jnp.where(lane < 96, jnp.concatenate([packed, tail], axis=0), 0.0)
    brick[0] = rows[:64].reshape(8, 8, LANES)
    brick[7] = rows[64:128].reshape(8, 8, LANES)
    brick[1:7, 0] = rows[128:176].reshape(6, 8, LANES)
    brick[1:7, 7] = rows[176:224].reshape(6, 8, LANES)
    brick[1:7, 1:7, 0] = rows[224:272].reshape(6, 8, LANES)[:, 1:7]
    brick[1:7, 1:7, 7] = rows[272:].reshape(6, 8, LANES)[:, 1:7]


def stacked(features, occupancy, neighbors, grad_output):
    depth = features.shape[0]

    def rows(block, first):
        return jnp.pad(block, ((first, STACK - first - block.shape[0]), (0, VOXELS - block.shape[1]))).astype(jnp.float32)

    return (
        rows(grad_output, 0) + rows(features, depth) + rows(occupancy, 2 * depth) + rows(neighbors, 2 * depth + 1)
    )


def pack_kernel(stack, packed, masked, cotangent_rows, masked_rows, brick):
    depth = masked.shape[0]
    side = stack[2 * depth:, :]
    occupied = side[0:1]
    for at, rows in ((0, cotangent_rows), (1, masked_rows)):
        product = stack[depth * at:depth * (at + 1), :] * occupied
        if at:
            masked[...] = product.astype(jnp.bfloat16)
        by_voxel = voxel_rows(product)
        rows[...] = by_voxel.astype(jnp.bfloat16)
        brick[at] = by_voxel.reshape(8, 8, 8, LANES)
        packed[SHELL * at:SHELL * (at + 1), :] = shell_of(brick.at[at]).astype(jnp.bfloat16)
    bricks = side[1:2, :LANES].astype(jnp.int32)
    lane = lax.broadcasted_iota(jnp.int32, (1, LANES), 1)
    own = jnp.sum(jnp.where(lane == 13, bricks, 0), axis=1, keepdims=True)
    codes = jnp.where(bricks == own, OWN, jnp.where(bricks == (own ^ 1), MATE, NEXT))
    codes = jnp.where(bricks < 0, NONE, codes).astype(jnp.float32)
    packed[2 * SHELL:, :] = jnp.broadcast_to(codes, (LANES, LANES)).T[:CODES].astype(jnp.bfloat16)


def faces(sign):
    if sign < 0:
        return slice(7, 8), slice(0, 1)
    if sign > 0:
        return slice(0, 1), slice(9, 10)
    return slice(0, 8), slice(1, 9)


def offset_id(x, y, z):
    return 9 * (x + 1) + 3 * (y + 1) + (z + 1)


def build_windows(bricks, weigh, columns, windows):
    for x in SIGNS:
        from_x, to_x = faces(x)
        for y in SIGNS:
            from_y, to_y = faces(y)
            parts = [brick[from_x, from_y] for brick in bricks]
            shape = parts[0].shape

            def side(z):
                return sum(part * scale for part, scale in zip(parts, weigh(x, y, z)))

            middle = parts[OWN] if x == 0 and y == 0 else side(0)
            middle = middle.reshape(-1, 8, LANES)
            below = side(-1).reshape(-1, 8, LANES)
            above = side(1).reshape(-1, 8, LANES)
            row = lax.broadcasted_iota(jnp.int32, middle.shape, 1)
            columns[0, to_x, to_y] = pltpu.roll(jnp.where(row == 7, below, middle), 1, 1).reshape(shape)
            columns[1, to_x, to_y] = middle.reshape(shape)
            columns[2, to_x, to_y] = pltpu.roll(jnp.where(row == 0, above, middle), 7, 1).reshape(shape)
    for dy in range(3):
        for dz in range(3):
            tap = 3 * dy + dz
            for px in range(10):
                windows[px, :, tap * LANES:(tap + 1) * LANES] = (
                    columns[dz, px, dy:dy + 8].reshape(64, LANES).astype(jnp.bfloat16)
                )


def bricks_of(own, mate, beyond, first, shells):
    shells[...] = jnp.zeros_like(shells)
    for at, ref in enumerate((mate, beyond)):
        fill_shell(shells.at[at], ref[first:first + SHELL, :].astype(jnp.float32))
    return [own[...].astype(jnp.float32).reshape(8, 8, 8, LANES), shells[0], shells[1]]


def codes_of(ref):
    return ref[2 * SHELL:, :].astype(jnp.float32)


def returned_scales(own, mate, beyond):
    tables = [codes_of(ref) for ref in (own, mate, beyond)]

    def weigh(x, y, z):
        at = offset_id(-x, -y, -z)
        return [jnp.where(table[at:at + 1] == code, 1.0, 0.0) for code, table in enumerate(tables)]

    return weigh


def read_scales(own):
    table = codes_of(own)

    def weigh(x, y, z):
        at = offset_id(x, y, z)
        return [jnp.where(table[at:at + 1] == code, 1.0, 0.0) for code in (OWN, MATE, NEXT)]

    return weigh


def span(windows, dx):
    return windows[dx:dx + 8].reshape(VOXELS, 9 * LANES)


def dense_rows(block):
    lane = lax.broadcasted_iota(jnp.int32, (72, LANES), 1)
    tail = jnp.concatenate([pltpu.roll(block[72:], 96 - 32 * third, 1) for third in range(3)], axis=0)
    return jnp.where(lane < 96, block[:72], tail)


def square_rows(dense, square):
    square[:72] = dense[:, :96]
    lane = lax.broadcasted_iota(jnp.int32, (24, LANES), 1)
    thirds = [pltpu.roll(dense[24 * third:24 * third + 24], 32 + 32 * third, 1) for third in range(3)]
    tail = jnp.where(lane < 32, thirds[0], jnp.where(lane < 64, thirds[1], thirds[2]))
    square[72:] = tail[:, :96]


def weight_grad_kernel(masked, own, mate, beyond, cotangent, grad, columns, windows, shells, dense):
    bricks = bricks_of(cotangent, mate, beyond, 0, shells)
    build_windows(bricks, returned_scales(own, mate, beyond), columns, windows)
    for dx in range(3):
        product = jnp.dot(masked[...], span(windows, dx), preferred_element_type=jnp.float32)
        for tap in range(9):
            at = 72 * (26 - (9 * dx + tap))
            dense[at:at + 72] = dense_rows(product[:, tap * LANES:(tap + 1) * LANES])
    dense[27 * 72:] = jnp.zeros((ROWS - 27 * 72, LANES), jnp.float32)
    grad[...] = dense[...].astype(jnp.bfloat16).reshape(grad.shape)


def sum_kernel(parts, copies):
    total = parts[0].astype(jnp.float32)
    for part in range(1, parts.shape[0]):
        total = total + parts[part].astype(jnp.float32)
    for copy in range(copies.shape[0]):
        copies[copy] = total.astype(copies.dtype)


def unpack_kernel(dense, grad):
    shares = [dense[GATHER.index(member)] for member in SCATTER]
    rows = jnp.concatenate(shares, axis=0).astype(jnp.float32)
    for tap in range(27):
        square_rows(rows[72 * tap:72 * tap + 72], grad.at[tap])


def outputs_kernel(
    occupancy, weight, own, mate, beyond, cotangent, masked,
    output, grad_features, columns, windows, shells, taps,
):
    depth = weight.shape[1]
    occupied = occupancy[...].astype(jnp.float32)
    taps[...] = jnp.zeros_like(taps)
    for tap in range(27):
        taps[tap, :depth, :depth] = weight[tap]

    def finish(rows):
        return (rows.T[:depth] * occupied).astype(jnp.bfloat16)

    bricks = bricks_of(masked, mate, beyond, SHELL, shells)
    build_windows(bricks, read_scales(own), columns, windows)
    total = jnp.zeros((VOXELS, LANES), jnp.float32)
    for dx in range(3):
        kernel = taps[9 * dx:9 * dx + 9].reshape(9 * LANES, LANES)
        total = total + jnp.dot(span(windows, dx), kernel, preferred_element_type=jnp.float32)
    output[0] = finish(total)

    bricks = bricks_of(cotangent, mate, beyond, 0, shells)
    build_windows(bricks, returned_scales(own, mate, beyond), columns, windows)
    total = jnp.zeros((VOXELS, LANES), jnp.float32)
    for dx in range(3):
        for tap in range(9):
            total = total + lax.dot_general(
                windows[dx:dx + 8, :, tap * LANES:(tap + 1) * LANES].reshape(VOXELS, LANES),
                taps[26 - (9 * dx + tap)],
                (((1,), (1,)), ((), ())),
                preferred_element_type=jnp.float32,
            )
    grad_features[0] = finish(total)


WINDOW_SCRATCH = [
    pltpu.VMEM((3, 10, 10, 8, LANES), jnp.float32),
    pltpu.VMEM((10, 64, 9 * LANES), jnp.bfloat16),
    pltpu.VMEM((2, 8, 8, 8, LANES), jnp.float32),
]


def neighbours(block):
    count = lax.axis_size("brick") * lax.axis_size("chan")
    beyond = lax.ppermute(block, AXES, [(i, i + 2 * (i % 2) - 1) for i in range(1, count - 1)])
    mate = lax.ppermute(block, AXES, [(i, i + 1 - 2 * (i % 2)) for i in range(count)])
    return mate, beyond


def call(kernel, name, shapes, operands, specs=None, scratch=(), flops=0, limit=LIMIT):
    return pl.pallas_call(
        kernel,
        out_shape=shapes,
        in_specs=specs or [VMEM] * len(operands),
        out_specs=jax.tree.map(lambda _: VMEM, shapes),
        scratch_shapes=list(scratch),
        compiler_params=pltpu.CompilerParams(vmem_limit_bytes=limit),
        cost_estimate=pl.CostEstimate(flops=flops, bytes_accessed=2 * 1024 * 1024, transcendentals=0),
        name=name,
    )(*operands)


def bf16(*shape):
    return jax.ShapeDtypeStruct(shape, jnp.bfloat16)


def near_groups(order):
    count = NEAR * FAR
    return [[first + member for member in order] for first in range(0, count, NEAR)]


def total_over_devices(grad):
    rows = grad.shape[1]
    far = [[first + NEAR * ((i + FIRST) % FAR) for i in range(FAR)] for first in range(NEAR)]
    pieces = lax.all_to_all(grad, AXES, 0, 0, tiled=True, axis_index_groups=near_groups(SCATTER))
    share = call(sum_kernel, "sum_near", bf16(FAR, rows, LANES), (pieces,))
    shares = lax.all_to_all(share, AXES, 0, 0, tiled=True, axis_index_groups=far)
    whole = call(sum_kernel, "sum_far", bf16(NEAR, rows, LANES), (shares,))
    return lax.all_to_all(whole, AXES, 0, 0, tiled=True, axis_index_groups=near_groups(GATHER))


def shards(features, occupancy, neighbors, weight, grad_output):
    depth = features.shape[1]
    stack = stacked(features[0], occupancy, neighbors, grad_output[0])
    own, masked, cotangent_rows, masked_rows = call(
        pack_kernel, "pack",
        [bf16(2 * SHELL + CODES, LANES), bf16(depth, VOXELS), bf16(VOXELS, LANES), bf16(VOXELS, LANES)],
        (stack,), scratch=[pltpu.VMEM((2, 8, 8, 8, LANES), jnp.float32)],
    )
    mate, beyond = neighbours(own)
    dot = 27 * 2 * LANES * LANES * VOXELS
    grad = call(
        weight_grad_kernel, "weight_grad", bf16(NEAR, ROWS // NEAR, LANES),
        (masked, own, mate, beyond, cotangent_rows),
        scratch=WINDOW_SCRATCH + [pltpu.VMEM((ROWS, LANES), jnp.float32)], flops=dot,
    )
    grad = total_over_devices(grad)
    output, grad_features = call(
        outputs_kernel, "outputs", [bf16(*features.shape)] * 2,
        (occupancy, weight, own, mate, beyond, cotangent_rows, masked_rows),
        scratch=WINDOW_SCRATCH + [pltpu.VMEM((27, LANES, LANES), jnp.bfloat16)], flops=2 * dot,
    )
    grad_weight = call(unpack_kernel, "unpack", jax.ShapeDtypeStruct((27, depth, depth), jnp.float32), (grad,))
    return output, grad_features, grad_weight


def solution(mesh):
    split = P(AXES, None, None)
    flat = P(AXES, None)
    return jax.shard_map(
        shards,
        mesh=mesh,
        in_specs=(split, flat, flat, P(), split),
        out_specs=(split, split, P()),
        check_vma=False,
    )
```

```python
import jax
import jax.numpy as jnp
from jax import lax
from jax.experimental import pallas as pl
from jax.experimental.pallas import tpu as pltpu
from jax.sharding import PartitionSpec as P

AXES = ("brick", "chan")
SIGNS = (-1, 0, 1)
VOXELS, LANES, CODES = 512, 128, 32
STACK = 200
SHELL = 240
ROWS = 2048
NEAR, FAR = 64, 8


def crossing(stride):
    chips = [(stride * j + 31) % 32 for j in range(32)]
    return [member for j in range(32) for member in (2 * chips[j] + 1, 2 * chips[-j])]


SCATTER = crossing(11)
GATHER = crossing(1)
FIRST = 4
OWN, MATE, NEXT, NONE = range(4)
VMEM = pl.BlockSpec(memory_space=pltpu.VMEM)
LIMIT = 32 * 1024 * 1024


def voxel_rows(block):
    spare = jnp.zeros((LANES - block.shape[0], block.shape[1]), jnp.float32)
    return jnp.concatenate([block, spare], axis=0).T


def shell_of(brick):
    pieces = [brick[0], brick[7], brick[1:7, 0], brick[1:7, 7], brick[1:7, :, 0], brick[1:7, :, 7]]
    rows = jnp.concatenate([piece.reshape(-1, LANES) for piece in pieces], axis=0)
    tail = jnp.concatenate([pltpu.roll(rows[SHELL:], 96 - 32 * at, 1) for at in range(3)], axis=0)
    lane = lax.broadcasted_iota(jnp.int32, (SHELL, LANES), 1)
    return jnp.where(lane < 96, rows[:SHELL], tail)


def fill_shell(brick, packed):
    third = SHELL // 3
    lane = lax.broadcasted_iota(jnp.int32, (third, LANES), 1)
    thirds = [pltpu.roll(packed[third * at:third * at + third], 32 + 32 * at, 1) for at in range(3)]
    tail = jnp.where(lane < 32, thirds[0], jnp.where(lane < 64, thirds[1], thirds[2]))
    lane = lax.broadcasted_iota(jnp.int32, (SHELL + third, LANES), 1)
    rows = jnp.where(lane < 96, jnp.concatenate([packed, tail], axis=0), 0.0)
    brick[0] = rows[:64].reshape(8, 8, LANES)
    brick[7] = rows[64:128].reshape(8, 8, LANES)
    brick[1:7, 0] = rows[128:176].reshape(6, 8, LANES)
    brick[1:7, 7] = rows[176:224].reshape(6, 8, LANES)
    brick[1:7, 1:7, 0] = rows[224:272].reshape(6, 8, LANES)[:, 1:7]
    brick[1:7, 1:7, 7] = rows[272:].reshape(6, 8, LANES)[:, 1:7]


def stacked(features, occupancy, neighbors, grad_output):
    depth = features.shape[0]

    def rows(block, first):
        return jnp.pad(block, ((first, STACK - first - block.shape[0]), (0, VOXELS - block.shape[1]))).astype(jnp.float32)

    return (
        rows(grad_output, 0) + rows(features, depth) + rows(occupancy, 2 * depth) + rows(neighbors, 2 * depth + 1)
    )


def pack_kernel(stack, packed, masked, cotangent_rows, masked_rows, brick):
    depth = masked.shape[0]
    side = stack[2 * depth:, :]
    occupied = side[0:1]
    for at, rows in ((0, cotangent_rows), (1, masked_rows)):
        product = stack[depth * at:depth * (at + 1), :] * occupied
        if at:
            masked[...] = product.astype(jnp.bfloat16)
        by_voxel = voxel_rows(product)
        rows[...] = by_voxel.astype(jnp.bfloat16)
        brick[at] = by_voxel.reshape(8, 8, 8, LANES)
        packed[SHELL * at:SHELL * (at + 1), :] = shell_of(brick.at[at]).astype(jnp.bfloat16)
    bricks = side[1:2, :LANES].astype(jnp.int32)
    lane = lax.broadcasted_iota(jnp.int32, (1, LANES), 1)
    own = jnp.sum(jnp.where(lane == 13, bricks, 0), axis=1, keepdims=True)
    codes = jnp.where(bricks == own, OWN, jnp.where(bricks == (own ^ 1), MATE, NEXT))
    codes = jnp.where(bricks < 0, NONE, codes).astype(jnp.float32)
    packed[2 * SHELL:, :] = jnp.broadcast_to(codes, (LANES, LANES)).T[:CODES].astype(jnp.bfloat16)


def faces(sign):
    if sign < 0:
        return slice(7, 8), slice(0, 1)
    if sign > 0:
        return slice(0, 1), slice(9, 10)
    return slice(0, 8), slice(1, 9)


def offset_id(x, y, z):
    return 9 * (x + 1) + 3 * (y + 1) + (z + 1)


def build_windows(bricks, weigh, columns, windows):
    for x in SIGNS:
        from_x, to_x = faces(x)
        for y in SIGNS:
            from_y, to_y = faces(y)
            parts = [brick[from_x, from_y] for brick in bricks]
            shape = parts[0].shape

            def side(z):
                return sum(part * scale for part, scale in zip(parts, weigh(x, y, z)))

            middle = parts[OWN] if x == 0 and y == 0 else side(0)
            middle = middle.reshape(-1, 8, LANES)
            below = side(-1).reshape(-1, 8, LANES)
            above = side(1).reshape(-1, 8, LANES)
            row = lax.broadcasted_iota(jnp.int32, middle.shape, 1)
            columns[0, to_x, to_y] = pltpu.roll(jnp.where(row == 7, below, middle), 1, 1).reshape(shape)
            columns[1, to_x, to_y] = middle.reshape(shape)
            columns[2, to_x, to_y] = pltpu.roll(jnp.where(row == 0, above, middle), 7, 1).reshape(shape)
    for dy in range(3):
        for dz in range(3):
            tap = 3 * dy + dz
            for px in range(10):
                windows[px, :, tap * LANES:(tap + 1) * LANES] = (
                    columns[dz, px, dy:dy + 8].reshape(64, LANES).astype(jnp.bfloat16)
                )


def bricks_of(own, mate, beyond, first, shells):
    shells[...] = jnp.zeros_like(shells)
    for at, ref in enumerate((mate, beyond)):
        fill_shell(shells.at[at], ref[first:first + SHELL, :].astype(jnp.float32))
    return [own[...].astype(jnp.float32).reshape(8, 8, 8, LANES), shells[0], shells[1]]


def codes_of(ref):
    return ref[2 * SHELL:, :].astype(jnp.float32)


def returned_scales(own, mate, beyond):
    tables = [codes_of(ref) for ref in (own, mate, beyond)]

    def weigh(x, y, z):
        at = offset_id(-x, -y, -z)
        return [jnp.where(table[at:at + 1] == code, 1.0, 0.0) for code, table in enumerate(tables)]

    return weigh


def read_scales(own):
    table = codes_of(own)

    def weigh(x, y, z):
        at = offset_id(x, y, z)
        return [jnp.where(table[at:at + 1] == code, 1.0, 0.0) for code in (OWN, MATE, NEXT)]

    return weigh


def span(windows, dx):
    return windows[dx:dx + 8].reshape(VOXELS, 9 * LANES)


def dense_rows(block):
    lane = lax.broadcasted_iota(jnp.int32, (72, LANES), 1)
    tail = jnp.concatenate([pltpu.roll(block[72:], 96 - 32 * third, 1) for third in range(3)], axis=0)
    return jnp.where(lane < 96, block[:72], tail)


def square_rows(dense, square):
    square[:72] = dense[:, :96]
    lane = lax.broadcasted_iota(jnp.int32, (24, LANES), 1)
    thirds = [pltpu.roll(dense[24 * third:24 * third + 24], 32 + 32 * third, 1) for third in range(3)]
    tail = jnp.where(lane < 32, thirds[0], jnp.where(lane < 64, thirds[1], thirds[2]))
    square[72:] = tail[:, :96]


def weight_grad_kernel(masked, own, mate, beyond, cotangent, grad, columns, windows, shells, dense):
    bricks = bricks_of(cotangent, mate, beyond, 0, shells)
    build_windows(bricks, returned_scales(own, mate, beyond), columns, windows)
    for dx in range(3):
        product = jnp.dot(masked[...], span(windows, dx), preferred_element_type=jnp.float32)
        for tap in range(9):
            at = 72 * (26 - (9 * dx + tap))
            dense[at:at + 72] = dense_rows(product[:, tap * LANES:(tap + 1) * LANES])
    dense[27 * 72:] = jnp.zeros((ROWS - 27 * 72, LANES), jnp.float32)
    grad[...] = dense[...].astype(jnp.bfloat16).reshape(grad.shape)


def sum_kernel(parts, copies):
    total = parts[0].astype(jnp.float32)
    for part in range(1, parts.shape[0]):
        total = total + parts[part].astype(jnp.float32)
    for copy in range(copies.shape[0]):
        copies[copy] = total.astype(copies.dtype)


def unpack_kernel(dense, grad):
    shares = [dense[GATHER.index(member)] for member in SCATTER]
    rows = jnp.concatenate(shares, axis=0).astype(jnp.float32)
    for tap in range(27):
        square_rows(rows[72 * tap:72 * tap + 72], grad.at[tap])


def outputs_kernel(
    occupancy, weight, own, mate, beyond, cotangent, masked,
    output, grad_features, columns, windows, shells, taps,
):
    depth = weight.shape[1]
    occupied = occupancy[...].astype(jnp.float32)
    taps[...] = jnp.zeros_like(taps)
    for tap in range(27):
        taps[tap, :depth, :depth] = weight[tap]

    def finish(rows):
        return (rows.T[:depth] * occupied).astype(jnp.bfloat16)

    bricks = bricks_of(masked, mate, beyond, SHELL, shells)
    build_windows(bricks, read_scales(own), columns, windows)
    total = jnp.zeros((VOXELS, LANES), jnp.float32)
    for dx in range(3):
        kernel = taps[9 * dx:9 * dx + 9].reshape(9 * LANES, LANES)
        total = total + jnp.dot(span(windows, dx), kernel, preferred_element_type=jnp.float32)
    output[0] = finish(total)

    bricks = bricks_of(cotangent, mate, beyond, 0, shells)
    build_windows(bricks, returned_scales(own, mate, beyond), columns, windows)
    total = jnp.zeros((VOXELS, LANES), jnp.float32)
    for dx in range(3):
        for tap in range(9):
            total = total + lax.dot_general(
                windows[dx:dx + 8, :, tap * LANES:(tap + 1) * LANES].reshape(VOXELS, LANES),
                taps[26 - (9 * dx + tap)],
                (((1,), (1,)), ((), ())),
                preferred_element_type=jnp.float32,
            )
    grad_features[0] = finish(total)


WINDOW_SCRATCH = [
    pltpu.VMEM((3, 10, 10, 8, LANES), jnp.float32),
    pltpu.VMEM((10, 64, 9 * LANES), jnp.bfloat16),
    pltpu.VMEM((2, 8, 8, 8, LANES), jnp.float32),
]


def neighbours(block):
    count = lax.axis_size("brick") * lax.axis_size("chan")
    beyond = lax.ppermute(block, AXES, [(i, i + 2 * (i % 2) - 1) for i in range(1, count - 1)])
    mate = lax.ppermute(block, AXES, [(i, i + 1 - 2 * (i % 2)) for i in range(count)])
    return mate, beyond


def call(kernel, name, shapes, operands, specs=None, scratch=(), flops=0, limit=LIMIT):
    return pl.pallas_call(
        kernel,
        out_shape=shapes,
        in_specs=specs or [VMEM] * len(operands),
        out_specs=jax.tree.map(lambda _: VMEM, shapes),
        scratch_shapes=list(scratch),
        compiler_params=pltpu.CompilerParams(vmem_limit_bytes=limit),
        cost_estimate=pl.CostEstimate(flops=flops, bytes_accessed=2 * 1024 * 1024, transcendentals=0),
        name=name,
    )(*operands)


def bf16(*shape):
    return jax.ShapeDtypeStruct(shape, jnp.bfloat16)


def near_groups(order):
    count = NEAR * FAR
    return [[first + member for member in order] for first in range(0, count, NEAR)]


def total_over_devices(grad):
    rows = grad.shape[1]
    far = [[first + NEAR * ((i + FIRST) % FAR) for i in range(FAR)] for first in range(NEAR)]
    pieces = lax.all_to_all(grad, AXES, 0, 0, tiled=True, axis_index_groups=near_groups(SCATTER))
    share = call(sum_kernel, "sum_near", bf16(FAR, rows, LANES), (pieces,))
    shares = lax.all_to_all(share, AXES, 0, 0, tiled=True, axis_index_groups=far)
    whole = call(sum_kernel, "sum_far", bf16(NEAR, rows, LANES), (shares,))
    return lax.all_to_all(whole, AXES, 0, 0, tiled=True, axis_index_groups=near_groups(GATHER))


def shards(features, occupancy, neighbors, weight, grad_output):
    depth = features.shape[1]
    stack = stacked(features[0], occupancy, neighbors, grad_output[0])
    own, masked, cotangent_rows, masked_rows = call(
        pack_kernel, "pack",
        [bf16(2 * SHELL + CODES, LANES), bf16(depth, VOXELS), bf16(VOXELS, LANES), bf16(VOXELS, LANES)],
        (stack,), scratch=[pltpu.VMEM((2, 8, 8, 8, LANES), jnp.float32)],
    )
    mate, beyond = neighbours(own)
    dot = 27 * 2 * LANES * LANES * VOXELS
    grad = call(
        weight_grad_kernel, "weight_grad", bf16(NEAR, ROWS // NEAR, LANES),
        (masked, own, mate, beyond, cotangent_rows),
        scratch=WINDOW_SCRATCH + [pltpu.VMEM((ROWS, LANES), jnp.float32)], flops=dot,
    )
    grad = total_over_devices(grad)
    output, grad_features = call(
        outputs_kernel, "outputs", [bf16(*features.shape)] * 2,
        (occupancy, weight, own, mate, beyond, cotangent_rows, masked_rows),
        scratch=WINDOW_SCRATCH + [pltpu.VMEM((27, LANES, LANES), jnp.bfloat16)], flops=2 * dot,
    )
    grad_weight = call(unpack_kernel, "unpack", jax.ShapeDtypeStruct((27, depth, depth), jnp.float32), (grad,))
    return output, grad_features, grad_weight


def solution(mesh):
    split = P(AXES, None, None)
    flat = P(AXES, None)
    return jax.shard_map(
        shards,
        mesh=mesh,
        in_specs=(split, flat, flat, P(), split),
        out_specs=(split, split, P()),
        check_vma=False,
    )
```
